32 devices in a mesh: rep: 4 (over y, x), fsdp: 8 (over z, core).
Axes of the slice: x: 2, y: 2, z: 4, core: 2. Of those that a mesh axis runs over, the one named last changes fastest.
Arguments:
- pixels: bfloat16 [32768, 6912], P(('rep', 'fsdp')), may hold values from -6 to 6
- image_class: int32 [32, 40], P(('rep', 'fsdp')), may hold values from 0 to 3, as said below
- resize_a: bfloat16 [64, 1024], replicated, may hold values from -0.75 to 0.75
- resize_b: bfloat16 [576, 1024], replicated, may hold values from -0.25 to 0.25
- resize_c: bfloat16 [2304, 1024], replicated, may hold values from -0.125 to 0.125
- posmap_a: bfloat16 [900, 49], replicated, may hold values from 0 to 0.3984375
- posmap_b: bfloat16 [100, 49], replicated, may hold values from 0 to 0.3984375
- posmap_c: bfloat16 [25, 49], replicated, may hold values from 0 to 0.3984375
- cotangent: bfloat16 [32768, 768], P(('rep', 'fsdp')), may hold values from -6 to 6
- patch_kernel: bfloat16 [3072, 768], P('fsdp'), may hold values from -0.109375 to 0.109375
- pos_table: bfloat16 [49, 768], P(None, 'fsdp'), may hold values from -3 to 3
- qkv_weight: bfloat16 [768, 2304], P('fsdp'), may hold values from -0.21875 to 0.21875
- out_weight: bfloat16 [768, 768], P('fsdp'), may hold values from -0.625 to 0.625
- up_weight: bfloat16 [768, 3072], P('fsdp'), may hold values from -0.21875 to 0.21875
- down_weight: bfloat16 [3072, 768], P('fsdp'), may hold values from -0.109375 to 0.109375
- biases: bfloat16 [7, 768], P(None, 'fsdp'), may hold values from -3 to 3
- up_bias: bfloat16 [3072], P('fsdp'), may hold values from -3 to 3
- gains: bfloat16 [2, 768], P(None, 'fsdp'), may hold values from 0.25 to 1.75
Outputs:
- output: bfloat16 [32768, 768], P(('rep', 'fsdp'))
- grad_pixels: bfloat16 [32768, 6912], P(('rep', 'fsdp'))
- grad_patch_kernel: float32 [3072, 768], P('fsdp')
- grad_pos_table: float32 [49, 768], P(None, 'fsdp')
- grad_qkv_weight: float32 [768, 2304], P('fsdp')
- grad_out_weight: float32 [768, 768], P('fsdp')
- grad_up_weight: float32 [768, 3072], P('fsdp')
- grad_down_weight: float32 [3072, 768], P('fsdp')
- grad_biases: float32 [7, 768], P(None, 'fsdp')
- grad_up_bias: float32 [3072], P('fsdp')
- grad_gains: float32 [2, 768], P(None, 'fsdp')
The draws below stay inside these ranges and needn't reach their ends.
Inputs may be any that keep to these rules, and one draw needn't show every extreme that they name: `image_class`: class 3 marks an empty slot; in each row the empty slots come after all images, the token counts of a row's images sum to at most 1024, class 0 stands only in slot 0, and row 0 holds a class 0 image.
All inputs are finite; a program needn't handle non-finite values.
Results may differ from the reference program's by a relative error of at most 0.018.
Values may be sent and summed in bfloat16 or wider, within the bound.
No kernel may reach another device: no remote copies, remote signals or barrier semaphores. Data moves between devices by JAX's collectives and lax.ppermute only.
A program may use at most 320 MiB of HBM per device.

```python
import jax
import jax.numpy as jnp
from jax import lax

D = 768
HEADS = 12
HEAD_DIM = 64
MLP = 3072
BASE = 32
PATCH_A = 8
PATCH_B = 24
PATCH_C = 48
TOK_DEV = 1024
GRID_A = 30
GRID_B = 10
GRID_C = 5
PIXELS = 6912
BASE_PIX = 3072
POS_CELLS = 49
IMG_DEV = 40
TOKENS = 32768
IMAGES = 1280


def draw_image_class(key, part):
    key = jax.random.fold_in(key, 7)
    first_key, pick_key = jax.random.split(key)
    device_rows = IMAGES // IMG_DEV
    leading = jax.random.randint(first_key, (device_rows,), 0, 4) == 0
    leading = leading.at[0].set(True)
    picks = jax.random.randint(pick_key, (device_rows, IMG_DEV), 1, 3).astype(jnp.int32)
    class_tokens = jnp.array([GRID_A * GRID_A, GRID_B * GRID_B, GRID_C * GRID_C, 0], dtype=jnp.int32)
    slot_ids = jnp.arange(IMG_DEV, dtype=jnp.int32)

    def place(remain, inputs):
        wanted_pick, slot = inputs
        wanted = jnp.where(jnp.logical_and(leading, slot == 0), 0, wanted_pick).astype(jnp.int32)
        fits = class_tokens[wanted] <= remain
        small_fits = class_tokens[2] <= remain
        placed = jnp.where(fits, wanted, jnp.where(small_fits, 2, 3)).astype(jnp.int32)
        return ((remain - class_tokens[placed]).astype(jnp.int32), placed)
    start_room = jnp.full((device_rows,), TOK_DEV, jnp.int32)
    _, placed = lax.scan(place, start_room, (picks.T, slot_ids))
    return placed.T.astype(jnp.int32)


def steps_of(own_key, dims, shards, low, high):
    gain = 1.0
    for axis_at, shards_of in shards:
        heights = jax.random.uniform(jax.random.fold_in(jax.random.fold_in(own_key, 6), axis_at), (shards_of,), jnp.float32, low / len(shards), high / len(shards))
        gain = gain * jnp.repeat(jnp.exp(heights), dims[axis_at] // shards_of).reshape((-1,) + (1,) * (len(dims) - 1 - axis_at))
    return gain


def noise(own_key, extent, scale, limit, shards=(), kind=jnp.bfloat16):
    values = jax.random.normal(own_key, extent, jnp.float32) * scale
    if len(shards) > 0:
        values = steps_of(own_key, extent, shards, -0.22, 0.18) * values
    return jnp.clip(values, min=-limit, max=limit).astype(kind)


def setup_inputs(seed: int = 0) -> dict:
    keys = jax.random.split(jax.random.key(seed), 19)
    pixels = noise(keys[0], (TOKENS, PIXELS), 1.0, 6.0, ((0, 32),))
    image_class = draw_image_class(jax.random.fold_in(keys[18], 71), 0)
    resize_a = noise(keys[2], (PATCH_A * PATCH_A, BASE * BASE), (PATCH_A * PATCH_A) ** -0.5, 0.75)
    resize_b = noise(keys[3], (PATCH_B * PATCH_B, BASE * BASE), (PATCH_B * PATCH_B) ** -0.5, 0.25)
    resize_c = noise(keys[4], (PATCH_C * PATCH_C, BASE * BASE), (PATCH_C * PATCH_C) ** -0.5, 0.125)
    posmap_a = jnp.clip(jax.random.uniform(keys[5], (GRID_A * GRID_A, POS_CELLS), jnp.float32, 0.0, 0.3984375), 0.0, 0.3984375).astype(jnp.bfloat16)
    posmap_b = jnp.clip(jax.random.uniform(keys[6], (GRID_B * GRID_B, POS_CELLS), jnp.float32, 0.0, 0.3984375), 0.0, 0.3984375).astype(jnp.bfloat16)
    posmap_c = jnp.clip(jax.random.uniform(keys[7], (GRID_C * GRID_C, POS_CELLS), jnp.float32, 0.0, 0.3984375), 0.0, 0.3984375).astype(jnp.bfloat16)
    cotangent = noise(keys[8], (TOKENS, D), 1.0, 6.0, ((0, 32),))
    patch_kernel = noise(keys[9], (BASE_PIX, D), BASE_PIX ** -0.5, 0.109375, ((0, 8),))
    pos_table = noise(keys[10], (POS_CELLS, D), 0.5, 3.0, ((1, 8),))
    qkv_weight = noise(keys[11], (D, 3 * D), D ** -0.5, 0.21875, ((0, 8),))
    out_weight = noise(keys[12], (D, D), (D // 8) ** -0.5, 0.625, ((0, 8),))
    up_weight = noise(keys[13], (D, MLP), D ** -0.5, 0.21875, ((0, 8),))
    down_weight = noise(keys[14], (MLP, D), MLP ** -0.5, 0.109375, ((0, 8),))
    biases = noise(keys[15], (7, D), 0.5, 3.0, ((1, 8),))
    up_bias = noise(keys[16], (MLP,), 0.5, 3.0, ((0, 8),))
    gains = jnp.clip(1.0 + 0.15 * jax.random.normal(keys[17], (2, D), jnp.float32), 0.25, 1.75).astype(jnp.bfloat16)
    return dict(pixels=pixels, image_class=image_class, resize_a=resize_a, resize_b=resize_b, resize_c=resize_c, posmap_a=posmap_a, posmap_b=posmap_b, posmap_c=posmap_c, cotangent=cotangent, patch_kernel=patch_kernel, pos_table=pos_table, qkv_weight=qkv_weight, out_weight=out_weight, up_weight=up_weight, down_weight=down_weight, biases=biases, up_bias=up_bias, gains=gains)


@jax.custom_vjp
def low(v):
    return lax.optimization_barrier(v.astype(jnp.bfloat16)).astype(jnp.float32)

@jax.custom_vjp
def low_back(v):
    return v

def low_keep(v):
    return (low(v), None)

def low_pass(kept, grad):
    return (grad,)

def back_keep(v):
    return (v, None)

def back_low(kept, grad):
    return (low(grad),)
low.defvjp(low_keep, low_pass)
low_back.defvjp(back_keep, back_low)
precise = lax.Precision.HIGHEST

def rounded_both(values):
    return low(low_back(values))

def product(left, right):
    return jnp.dot(left, right, precision=precise)

def token_layout(classes, tokens_here):
    class_tokens = jnp.array([GRID_A * GRID_A, GRID_B * GRID_B, GRID_C * GRID_C, 0], dtype=jnp.int32)
    class_ids = jnp.arange(4, dtype=jnp.int32)
    image_tokens = lax.optimization_barrier(jnp.sum(jnp.where(classes[:, None] == class_ids[None, :], class_tokens[None, :], 0), axis=1)).astype(jnp.int32)
    image_ends = jnp.cumsum(image_tokens).astype(jnp.int32)
    image_starts = (image_ends - image_tokens).astype(jnp.int32)
    positions = jnp.arange(tokens_here, dtype=jnp.int32)
    segment = lax.optimization_barrier(jnp.sum((image_ends[None, :] <= positions[:, None]).astype(jnp.int32), axis=1)).astype(jnp.int32)
    membership = segment[:, None] == jnp.arange(classes.shape[0], dtype=jnp.int32)[None, :]
    live_rows = jnp.any(membership, axis=1)
    category = (lax.optimization_barrier(jnp.sum(jnp.where(membership, classes[None, :], 0), axis=1)) + jnp.where(live_rows, 0, 3)).astype(jnp.int32)
    offset = (positions - lax.optimization_barrier(jnp.sum(jnp.where(membership, image_starts[None, :], 0), axis=1))).astype(jnp.int32)
    return (segment, category, offset, live_rows)

def position_rows(category, offset, tables):
    rows_out = jnp.zeros((category.shape[0], tables[0].shape[1]), jnp.float32)
    for class_id, table_rows in enumerate(tables):
        row_index = jnp.clip(offset, 0, table_rows.shape[0] - 1).astype(jnp.int32)
        picked = jnp.take(table_rows, row_index, axis=0).astype(jnp.float32)
        rows_out = rows_out + jnp.where((category == class_id)[:, None], picked, 0.0)
    return rows_out

def layer_norm(values, gain_row, shift_row):
    center = values - lax.optimization_barrier(jnp.mean(values, axis=-1, keepdims=True))
    spread = lax.optimization_barrier(jnp.mean(center * center, axis=-1, keepdims=True))
    return center * lax.rsqrt(spread + 1e-06) * gain_row + shift_row

def attend(query_heads, key_heads, value_heads, segment):
    scores = jnp.einsum('qhd,khd->hqk', query_heads, key_heads, precision=precise) * HEAD_DIM ** (-0.5)
    same_image = segment[:, None] == segment[None, :]
    scores = low_back(jnp.where(same_image[None], scores, -1e+30))
    row_max = lax.optimization_barrier(jnp.max(scores, axis=-1, keepdims=True))
    weights = jnp.exp(scores - row_max)
    probs = low(weights / lax.optimization_barrier(jnp.sum(weights, axis=-1, keepdims=True)))
    return jnp.einsum('hqk,khd->qhd', probs, value_heads, precision=precise)

def forward_block(pixel_rows, classes, weights, matrices, tables):
    kernel, pos_weight, qkv_proj, out_proj, up_proj, down_proj, bias_rows, up_shift, gain_rows = weights
    tokens_here = pixel_rows.shape[0]
    segment, category, offset, live_rows = token_layout(classes, tokens_here)
    pixel_frame = pixel_rows.reshape(tokens_here, 3, -1)
    resized = jnp.zeros((tokens_here, 3, matrices[0].shape[1]), jnp.float32)
    for class_id, matrix in enumerate(matrices):
        area = matrix.shape[0]
        partial_rows = jnp.einsum('tcp,pk->tck', pixel_frame[:, :, :area], matrix, precision=precise)
        resized = resized + jnp.where((category == class_id)[:, None, None], partial_rows, 0.0)
    resized = rounded_both(resized.reshape(tokens_here, -1))
    pos_rows = position_rows(category, offset, tables)
    embed = low_back(product(resized, kernel) + bias_rows[0] + product(pos_rows, pos_weight))
    normed1 = low(layer_norm(embed, gain_rows[0], bias_rows[1]))
    features = embed.shape[1]
    shift_vec = jnp.concatenate([bias_rows[2], jnp.zeros_like(bias_rows[2]), bias_rows[3]])
    projected = rounded_both(product(normed1, qkv_proj) + shift_vec)
    split_heads = projected.reshape(tokens_here, 3, HEADS, HEAD_DIM)
    mixed = rounded_both(attend(split_heads[:, 0], split_heads[:, 1], split_heads[:, 2], segment).reshape(tokens_here, features))
    hidden = embed + low_back(product(mixed, out_proj) + bias_rows[4])
    normed2 = low(layer_norm(hidden, gain_rows[1], bias_rows[5]))
    pre_act = low_back(product(normed2, up_proj) + up_shift)
    act = low(jax.nn.gelu(pre_act, approximate=True))
    result = hidden + low_back(product(act, down_proj) + bias_rows[6])
    return result * live_rows[:, None].astype(jnp.float32)

def reference(pixels, image_class, resize_a, resize_b, resize_c, posmap_a, posmap_b, posmap_c, cotangent, patch_kernel, pos_table, qkv_weight, out_weight, up_weight, down_weight, biases, up_bias, gains):
    weights = tuple((weight_in.astype(jnp.float32) for weight_in in (patch_kernel, pos_table, qkv_weight, out_weight, up_weight, down_weight, biases, up_bias, gains)))
    matrices = (resize_a.astype(jnp.float32), resize_b.astype(jnp.float32), resize_c.astype(jnp.float32))
    tables = (posmap_a, posmap_b, posmap_c)
    blocks = pixels.shape[0] // TOK_DEV
    pixel_blocks = pixels.astype(jnp.float32).reshape(blocks, TOK_DEV, PIXELS)

    def forward_all(pixel_input, weight_input):

        def one_block(inputs):
            return forward_block(inputs[0], inputs[1], weight_input, matrices, tables)
        return lax.map(jax.checkpoint(one_block), (pixel_input, image_class))
    result, pullback = jax.vjp(forward_all, pixel_blocks, weights)
    grad_pix, grad_weights = pullback(cotangent.astype(jnp.float32).reshape(blocks, TOK_DEV, D))
    return (result.reshape(-1, D).astype(jnp.bfloat16), grad_pix.reshape(-1, PIXELS).astype(jnp.bfloat16), grad_weights[0], grad_weights[1], grad_weights[2], grad_weights[3], grad_weights[4], grad_weights[5], grad_weights[6], grad_weights[7], grad_weights[8])
```

```python
import jax
import jax.numpy as jnp
from jax import lax
from jax.experimental import pallas as pl
from jax.experimental.pallas import tpu as pltpu
from jax.sharding import PartitionSpec as P

HEADS = 12
GRID_A = 30
GRID_B = 10
GRID_C = 5
CHUNK = 16
TILE = 256
F32 = jnp.float32
BF16 = jnp.bfloat16
NEG = -1e30
VMEM = 60 * 1024 * 1024


def nt(a, b):
    return lax.dot_general(a, b, (((1,), (1,)), ((), ())), preferred_element_type=F32)


def nn(a, b):
    return lax.dot_general(a, b, (((1,), (0,)), ((), ())), preferred_element_type=F32)


def tn(a, b):
    return lax.dot_general(a, b, (((0,), (0,)), ((), ())), preferred_element_type=F32)


def params(**more):
    return pltpu.CompilerParams(vmem_limit_bytes=VMEM, **more)


def cost(flops, moved, exps=0):
    return pl.CostEstimate(flops=int(flops), bytes_accessed=int(moved), transcendentals=int(exps))


def token_layout(classes, tokens_here):
    class_tokens = jnp.array(
        [GRID_A * GRID_A, GRID_B * GRID_B, GRID_C * GRID_C, 0], dtype=jnp.int32
    )
    class_ids = jnp.arange(4, dtype=jnp.int32)
    image_tokens = jnp.sum(
        jnp.where(classes[:, None] == class_ids[None, :], class_tokens[None, :], 0), axis=1
    )
    image_ends = jnp.cumsum(image_tokens)
    image_starts = image_ends - image_tokens
    positions = jnp.arange(tokens_here, dtype=jnp.int32)
    segment = jnp.sum((image_ends[None, :] <= positions[:, None]).astype(jnp.int32), axis=1)
    membership = segment[:, None] == jnp.arange(classes.shape[0], dtype=jnp.int32)[None, :]
    live_rows = jnp.any(membership, axis=1)
    category = jnp.sum(jnp.where(membership, classes[None, :], 0), axis=1) + jnp.where(
        live_rows, 0, 3
    )
    offset = positions - jnp.sum(jnp.where(membership, image_starts[None, :], 0), axis=1)
    return (segment, category, offset, live_rows)


def chunk_lists(category):
    chunks = category.reshape(-1, CHUNK)
    here = jnp.any(chunks[None, :, :] == jnp.arange(3, dtype=jnp.int32)[:, None, None], axis=2)
    place = jnp.cumsum(here.astype(jnp.int32), axis=1) - 1
    count = chunks.shape[0]
    ids = jnp.arange(count, dtype=jnp.int32)
    hit = here[:, :, None] & (place[:, :, None] == ids[None, None, :])
    listed = jnp.sum(jnp.where(hit, ids[None, :, None], 0), axis=1)
    return jnp.concatenate([place[:, -1:] + 1, listed], axis=1).astype(jnp.int32)


def resize_rows(lists, cat_ref, src_ref, out_ref, lhs, class_id, width, product, columns):
    number = lists[class_id, 0]

    @pl.loop(0, (number + TILE // CHUNK - 1) // (TILE // CHUNK))
    def _(t):
        base = t * (TILE // CHUNK)
        for u in range(TILE // CHUNK):
            row = pl.multiple_of(lists[class_id, 1 + jnp.minimum(base + u, number - 1)] * CHUNK, CHUNK)
            lhs[u * CHUNK : (u + 1) * CHUNK, 0:width] = src_ref[pl.ds(row, CHUNK), 0:width]
        total = product(lhs[:, 0:width])
        for u in range(TILE // CHUNK):

            @pl.when(base + u < number)
            def _():
                row = pl.multiple_of(lists[class_id, 1 + base + u] * CHUNK, CHUNK)
                mine = cat_ref[pl.ds(row, CHUNK), :] == class_id
                old = out_ref[pl.ds(row, CHUNK), 0:columns].astype(F32)
                new = total[u * CHUNK : (u + 1) * CHUNK, :]
                out_ref[pl.ds(row, CHUNK), 0:columns] = jnp.where(mine, new, old).astype(
                    out_ref.dtype
                )


def resize_kernel(lists, px_ref, cat_ref, ra_ref, rb_ref, rc_ref, out_ref, lhs):
    out_ref[...] = jnp.zeros_like(out_ref)
    for class_id, matrix in enumerate((ra_ref, rb_ref, rc_ref)):
        resize_rows(
            lists, cat_ref, px_ref, out_ref, lhs, class_id, matrix.shape[0],
            lambda rows, matrix=matrix: nn(rows, matrix[...]), matrix.shape[1],
        )


def resize(lists, pixels, category, ra, rb, rc):
    tokens, wide = pixels.shape
    area = wide // 3
    base = rc.shape[1]
    whole = lambda a: pl.BlockSpec(a.shape, lambda c, s: (0, 0))
    return pl.pallas_call(
        resize_kernel,
        grid_spec=pltpu.PrefetchScalarGridSpec(
            num_scalar_prefetch=1,
            grid=(3,),
            in_specs=[pl.BlockSpec((tokens, area), lambda c, s: (0, c)), whole(category), whole(ra), whole(rb), whole(rc)],
            out_specs=pl.BlockSpec((tokens, base), lambda c, s: (0, c)),
            scratch_shapes=[pltpu.VMEM((TILE, area), BF16)],
        ),
        out_shape=jax.ShapeDtypeStruct((tokens, 3 * base), BF16),
        compiler_params=params(),
        cost_estimate=cost(tokens * 3 * base * 1200 * 2, tokens * wide * 2 + tokens * base * 6),
        name="resize",
    )(lists, pixels, category, ra, rb, rc)


def unresize_kernel(lists, g_ref, w_ref, cat_ref, ra_ref, rb_ref, rc_ref, out_ref, grow, lhs):
    tokens = g_ref.shape[0]
    out_ref[...] = jnp.zeros_like(out_ref)

    @pl.loop(0, tokens // TILE)
    def _(t):
        rows = pl.ds(pl.multiple_of(t * TILE, TILE), TILE)
        grow[rows, :] = nt(g_ref[rows, :], w_ref[0, 0]).astype(BF16)

    for class_id, matrix in enumerate((ra_ref, rb_ref, rc_ref)):
        resize_rows(
            lists, cat_ref, grow, out_ref, lhs, class_id, grow.shape[1],
            lambda rows, matrix=matrix: nt(rows, matrix[...]), matrix.shape[0],
        )


def unresize(lists, g_emb, groups, category, ra, rb, rc, area):
    tokens, width = g_emb.shape
    base = rc.shape[1]
    whole = lambda a: pl.BlockSpec(a.shape, lambda c, s: (0, 0))
    kernels = groups.reshape(4, 3, base, width)
    return pl.pallas_call(
        unresize_kernel,
        grid_spec=pltpu.PrefetchScalarGridSpec(
            num_scalar_prefetch=1,
            grid=(3,),
            in_specs=[
                whole(g_emb), pl.BlockSpec((1, 1, base, width), lambda c, s: (0, c, 0, 0)),
                whole(category), whole(ra), whole(rb), whole(rc),
            ],
            out_specs=pl.BlockSpec((tokens, area), lambda c, s: (0, c)),
            scratch_shapes=[pltpu.VMEM((tokens, base), BF16), pltpu.VMEM((TILE, base), BF16)],
        ),
        out_shape=jax.ShapeDtypeStruct((tokens, 3 * area), BF16),
        compiler_params=params(),
        cost_estimate=cost(tokens * 3 * base * 2000 * 2, tokens * area * 6 + tokens * base * 6),
        name="unresize",
    )(lists, g_emb, kernels, category, ra, rb, rc)


def norm_parts(values):
    center = values - jnp.mean(values, axis=-1, keepdims=True)
    rstd = lax.rsqrt(jnp.mean(center * center, axis=-1, keepdims=True) + 1e-06)
    return center * rstd, rstd


def norm_back(xhat, rstd, grad, gain):
    dxhat = grad * gain
    return rstd * (
        dxhat
        - jnp.mean(dxhat, axis=-1, keepdims=True)
        - xhat * jnp.mean(dxhat * xhat, axis=-1, keepdims=True)
    )


def square(ref):
    value = ref[...]
    return value.reshape(-1, value.shape[-1])


def row_tiles(tokens, body):
    @pl.loop(0, tokens // TILE)
    def _(t):
        body(pl.ds(pl.multiple_of(t * TILE, TILE), TILE))


def embed_kernel(res_ref, kern_ref, qkv_ref, pos_ref, table_ref, small_ref, embed_ref, norm_ref, proj_ref):
    step = pl.program_id(0)
    tokens = res_ref.shape[0]

    @pl.when(step == 0)
    def _():
        def body(rows):
            embed_ref[rows, :] = (
                nn(res_ref[rows, :], square(kern_ref)) + small_ref[0:1, :] + nn(pos_ref[rows, :], table_ref[...])
            )

        row_tiles(tokens, body)

    @pl.when((step > 0) & (step < 4))
    def _():
        def body(rows):
            embed_ref[rows, :] += nn(res_ref[rows, :], square(kern_ref))

        row_tiles(tokens, body)

    @pl.when(step == 3)
    def _():
        def body(rows):
            xhat, _ = norm_parts(embed_ref[rows, :])
            norm_ref[rows, :] = (xhat * small_ref[7:8, :] + small_ref[1:2, :]).astype(BF16)

        row_tiles(tokens, body)

    @pl.when(step >= 4)
    def _():
        shift = jnp.where(
            step == 4, small_ref[2:3, :], jnp.where(step == 6, small_ref[3:4, :], jnp.zeros_like(small_ref[3:4, :]))
        )

        def body(rows):
            proj_ref[rows, :] = (nn(norm_ref[rows, :], square(qkv_ref)) + shift).astype(BF16)

        row_tiles(tokens, body)


def embed_call(resized, rowwise, colwise, pos_rows, table, small):
    tokens = resized.shape[0]
    width = small.shape[1]
    bands, deep = colwise.shape[1], colwise.shape[3]
    whole = lambda a: pl.BlockSpec(a.shape, lambda s: (0, 0))
    fixed = pl.BlockSpec((tokens, width), lambda s: (0, 0))
    return pl.pallas_call(
        embed_kernel,
        grid=(7,),
        in_specs=[
            pl.BlockSpec((tokens, width), lambda s: (0, jnp.minimum(s, 3))),
            pl.BlockSpec((1, 1, width, width), lambda s: (0, jnp.minimum(s, 3), 0, 0)),
            pl.BlockSpec((1, bands, 1, deep, width), lambda s: (1, 0, jnp.maximum(s - 4, 0), 0, 0)),
            whole(pos_rows), whole(table), whole(small),
        ],
        out_specs=[fixed, fixed, pl.BlockSpec((tokens, width), lambda s: (0, jnp.maximum(s - 4, 0)))],
        out_shape=[
            jax.ShapeDtypeStruct((tokens, width), F32),
            jax.ShapeDtypeStruct((tokens, width), BF16),
            jax.ShapeDtypeStruct((tokens, 3 * width), BF16),
        ],
        compiler_params=params(),
        cost_estimate=cost(7 * 2 * tokens * width * width, tokens * width * 20 + 7 * width * width * 2),
        name="embed",
    )(resized, rowwise, colwise, pos_rows, table, small)


def attend_kernel(dense_ref, q_ref, k_ref, v_ref, oh_ref, km_ref, o_ref, lse_ref, kaug, vaug):
    tokens = q_ref.shape[0]
    lane = lax.broadcasted_iota(jnp.int32, (1, 128), 1)
    kaug[:, 0:128] = k_ref[...]
    kaug[:, 128:256] = km_ref[...]
    vaug[:, 0:128] = v_ref[...]
    vaug[:, 128:256] = jnp.ones((tokens, 128), BF16)

    def tile(rows, cols):
        q = q_ref[rows, :] * jnp.asarray(0.125, BF16)
        oh = oh_ref[rows, :]
        keys, vals = kaug[cols, :], vaug[cols, :]
        outs, logs = [], []
        for h in range(2):
            mine = (lane < 64) if h == 0 else (lane >= 64)
            left = jnp.concatenate([jnp.where(mine, q, jnp.zeros_like(q)), oh], axis=1)
            scores = nt(left, keys)
            top = jnp.max(scores, axis=1, keepdims=True)
            weights = jnp.exp(scores - top).astype(BF16)
            both = nn(weights, vals)
            total = both[:, 128:256]
            outs.append(both[:, 0:128] / total)
            logs.append(top + jnp.log(total))
        o_ref[rows, :] = jnp.where(lane < 64, outs[0], outs[1]).astype(o_ref.dtype)
        lse_ref[rows, :] = jnp.where(lane < 64, logs[0], logs[1])

    attend_tiles(dense_ref, tokens, tile)


def attend_tiles(dense_ref, tokens, tile):
    @pl.when(dense_ref[0] != 0)
    def _():
        @pl.loop(0, tokens // TILE)
        def _(t):
            tile(pl.ds(pl.multiple_of(t * TILE, TILE), TILE), pl.ds(0, tokens))

    @pl.when(dense_ref[0] == 0)
    def _():
        @pl.loop(0, tokens // TILE)
        def _(t):
            first = pl.multiple_of(jnp.clip(t * TILE - 128, 0, tokens - 512), 128)
            tile(pl.ds(pl.multiple_of(t * TILE, TILE), TILE), pl.ds(first, 512))


def attend(dense, projected, onehot, keymask):
    tokens = projected.shape[0]
    pairs = projected.shape[1] // 3 // 128
    part = lambda at: pl.BlockSpec((tokens, 128), lambda j, d: (0, at + j))
    whole = pl.BlockSpec((tokens, 128), lambda j, d: (0, 0))
    return pl.pallas_call(
        attend_kernel,
        grid_spec=pltpu.PrefetchScalarGridSpec(
            num_scalar_prefetch=1,
            grid=(pairs,),
            in_specs=[part(0), part(pairs), part(2 * pairs), whole, whole],
            out_specs=[part(0), part(0)],
            scratch_shapes=[pltpu.VMEM((tokens, 256), BF16), pltpu.VMEM((tokens, 256), BF16)],
        ),
        out_shape=[
            jax.ShapeDtypeStruct((tokens, pairs * 128), BF16),
            jax.ShapeDtypeStruct((tokens, pairs * 128), F32),
        ],
        compiler_params=params(),
        cost_estimate=cost(2 * 2 * 12 * tokens * tokens * 256, tokens * 2304 * 2 + tokens * 768 * 6, 12 * tokens * tokens),
        name="attend",
    )(dense, projected, projected, projected, onehot, keymask)


def split3(x):
    high = x.astype(BF16)
    rest = x - high.astype(F32)
    middle = rest.astype(BF16)
    low = (rest - middle.astype(F32)).astype(BF16)
    return high, middle, low


def attend_back_kernel(
    dense_ref, q_ref, k_ref, v_ref, g_ref, o_ref, lse_ref, oh_ref, km_ref, out_ref, kaug, vaug, dkeys, dvals
):
    tokens = q_ref.shape[0]
    lane = lax.broadcasted_iota(jnp.int32, (1, 128), 1)
    kaug[:, 0:128] = k_ref[...]
    kaug[:, 128:256] = km_ref[...]
    vaug[:, 0:128] = v_ref[...]
    vaug[:, 128:256] = jnp.broadcast_to(jnp.where(lane < 3, -1.0, 0.0).astype(BF16), (tokens, 128))
    dkeys[...] = jnp.zeros_like(dkeys)
    dvals[...] = jnp.zeros_like(dvals)

    def put(parts, at, other):
        for i, piece in enumerate(parts):
            other = jnp.where(lane == at + i, piece, other)
        return other

    def tile(rows, cols):
        q = q_ref[rows, :] * jnp.asarray(0.125, BF16)
        g = g_ref[rows, :]
        oh = oh_ref[rows, :]
        go = g.astype(F32) * o_ref[rows, :].astype(F32)
        lse = lse_ref[rows, :]
        keys, vals = kaug[cols, :], vaug[cols, :]
        plain = keys[:, 0:128]
        dqs, dkt, dvt = [], None, None
        for h in range(2):
            mine = (lane < 64) if h == 0 else (lane >= 64)
            delta = jnp.sum(jnp.where(mine, go, 0.0), axis=1, keepdims=True)
            qm = jnp.where(mine, q, jnp.zeros_like(q))
            gm = jnp.where(mine, g, jnp.zeros_like(g))
            qa = jnp.concatenate([qm, put(split3(lse[:, 64 * h : 64 * h + 1]), 64, oh)], axis=1)
            ga = jnp.concatenate([gm, put(split3(delta), 0, jnp.zeros_like(oh))], axis=1)
            probs = jnp.exp(nt(keys, qa))
            dscores = (probs * nt(vals, ga)).astype(BF16)
            a, b = nn(probs.astype(BF16), gm), nn(dscores, qm)
            dvt = a if dvt is None else dvt + a
            dkt = b if dkt is None else dkt + b
            dqs.append(tn(dscores, plain))
        out_ref[0, rows, :] = (jnp.where(lane < 64, dqs[0], dqs[1]) * 0.125).astype(BF16)
        dkeys[cols, :] += dkt
        dvals[cols, :] += dvt

    attend_tiles(dense_ref, tokens, tile)
    out_ref[1] = dkeys[...].astype(BF16)
    out_ref[2] = dvals[...].astype(BF16)


def attend_back(dense, projected, g_mixed, mixed, lse, onehot, keymask):
    tokens = projected.shape[0]
    pairs = projected.shape[1] // 3 // 128
    part = lambda at: pl.BlockSpec((tokens, 128), lambda j, d: (0, at + j))
    whole = pl.BlockSpec((tokens, 128), lambda j, d: (0, 0))
    return pl.pallas_call(
        attend_back_kernel,
        grid_spec=pltpu.PrefetchScalarGridSpec(
            num_scalar_prefetch=1,
            grid=(pairs,),
            in_specs=[part(0), part(pairs), part(2 * pairs), part(0), part(0), part(0), whole, whole],
            out_specs=pl.BlockSpec((3, tokens, 128), lambda j, d: (0, 0, j)),
            scratch_shapes=[
                pltpu.VMEM((tokens, 256), BF16), pltpu.VMEM((tokens, 256), BF16),
                pltpu.VMEM((tokens, 128), F32), pltpu.VMEM((tokens, 128), F32),
            ],
        ),
        out_shape=jax.ShapeDtypeStruct((3, tokens, pairs * 128), BF16),
        compiler_params=params(),
        cost_estimate=cost(5 * 2 * 12 * tokens * tokens * 256, tokens * 768 * 22, 12 * tokens * tokens),
        name="attend_back",
    )(dense, projected, projected, projected, g_mixed, mixed, lse, onehot, keymask)


def mlp_kernel(
    embed_ref, mixed_ref, cot_ref, live_ref, small_ref, shift_ref, wo_ref, up_ref, down_ref,
    out_ref, ghid_ref, gmixed_ref, gdown_ref, gup_ref, gwo_ref, sums_ref, gshift_ref,
    hidden, xhats, norm2, gbranch, total, gnorm, act, gpre,
):
    step = pl.program_id(0)
    tokens = embed_ref.shape[0]

    @pl.when(step == 0)
    def _():
        def body(rows):
            value = embed_ref[rows, :] + nn(mixed_ref[rows, :], square(wo_ref)) + small_ref[4:5, :]
            hidden[rows, :] = value
            total[rows, :] = value + small_ref[6:7, :]
            xhat, _ = norm_parts(value)
            norm2[rows, :] = (xhat * small_ref[8:9, :] + small_ref[5:6, :]).astype(BF16)
            gbranch[rows, :] = (cot_ref[rows, :].astype(F32) * live_ref[rows, :]).astype(BF16)
            gnorm[rows, :] = jnp.zeros((TILE, gnorm.shape[1]), F32)

        row_tiles(tokens, body)

    up, down = square(up_ref), square(down_ref)

    def body(rows):
        x = nn(norm2[rows, :], up) + shift_ref[0]
        square_x = x * x
        t = jnp.tanh(0.7978845608028654 * (x + 0.044715 * (square_x * x)))
        half = 0.5 * (1.0 + t)
        acts = (x * half).astype(BF16)
        act[rows, :] = acts
        total[rows, :] += nn(acts, down)
        slope = half + 0.5 * x * (1.0 - t * t) * (
            0.7978845608028654 + (0.7978845608028654 * 3 * 0.044715) * square_x
        )
        gp = (nt(gbranch[rows, :], down) * slope).astype(BF16)
        gpre[rows, :] = gp
        gnorm[rows, :] += nt(gp, up)

    row_tiles(tokens, body)
    gdown_ref[0] = tn(act[...], gbranch[...]).astype(BF16)
    gup_ref[...] = tn(norm2[...], gpre[...]).astype(BF16).reshape(gup_ref.shape)
    gshift_ref[0] = jnp.sum(gpre[...].astype(F32), axis=0, keepdims=True)

    @pl.when(step == 3)
    def _():
        sums_ref[...] = jnp.zeros_like(sums_ref)
        wo = square(wo_ref)

        def body(rows):
            out_ref[rows, :] = (total[rows, :] * live_ref[rows, :]).astype(BF16)
            xhat, rstd = norm_parts(hidden[rows, :])
            grad = gnorm[rows, :]
            gout = gbranch[rows, :].astype(F32)
            ghid = gout + norm_back(xhat, rstd, grad, small_ref[8:9, :])
            ghid_ref[rows, :] = ghid
            gmix = ghid.astype(BF16)
            xhats[rows, :] = gmix
            gmixed_ref[rows, :] = nt(gmix, wo).astype(BF16)
            sums_ref[4:5, :] += jnp.sum(gmix.astype(F32), axis=0, keepdims=True)
            sums_ref[5:6, :] += jnp.sum(grad, axis=0, keepdims=True)
            sums_ref[6:7, :] += jnp.sum(gout, axis=0, keepdims=True)
            sums_ref[8:9, :] += jnp.sum(grad * xhat, axis=0, keepdims=True)

        row_tiles(tokens, body)
        gwo_ref[...] = tn(mixed_ref[...], xhats[...]).astype(BF16).reshape(gwo_ref.shape)


def mlp_call(embed, mixed, cotangent, live, small, shift, rowwise, colwise):
    tokens, width = embed.shape
    bands, deep = colwise.shape[1], colwise.shape[3]
    fixed = pl.BlockSpec((tokens, width), lambda s: (0, 0))
    whole = lambda a: pl.BlockSpec(a.shape, lambda s: (0, 0))
    band = lambda group, at: pl.BlockSpec((1, bands, 1, deep, width), lambda s: (group, 0, at(s), 0, 0))
    scratch = lambda kind: pltpu.VMEM((tokens, width), kind)
    return pl.pallas_call(
        mlp_kernel,
        grid=(4,),
        in_specs=[
            fixed, fixed, fixed, whole(live), whole(small),
            pl.BlockSpec((1, 1, width), lambda s: (s, 0, 0)),
            band(1, lambda s: 3), band(2, lambda s: s),
            pl.BlockSpec((1, 1, width, width), lambda s: (3, s, 0, 0)),
        ],
        out_specs=[
            fixed, fixed, fixed,
            pl.BlockSpec((1, width, width), lambda s: (s, 0, 0)),
            pl.BlockSpec((bands, 1, deep, width), lambda s: (0, s, 0, 0)),
            pl.BlockSpec((bands, deep, width), lambda s: (0, 0, 0)),
            pl.BlockSpec((16, width), lambda s: (0, 0)),
            pl.BlockSpec((1, 1, width), lambda s: (s, 0, 0)),
        ],
        out_shape=[
            jax.ShapeDtypeStruct((tokens, width), BF16),
            jax.ShapeDtypeStruct((tokens, width), F32),
            jax.ShapeDtypeStruct((tokens, width), BF16),
            jax.ShapeDtypeStruct((4, width, width), BF16),
            jax.ShapeDtypeStruct((bands, 4, deep, width), BF16),
            jax.ShapeDtypeStruct((bands, deep, width), BF16),
            jax.ShapeDtypeStruct((16, width), F32),
            jax.ShapeDtypeStruct((4, 1, width), F32),
        ],
        scratch_shapes=[
            scratch(F32), scratch(BF16), scratch(BF16), scratch(BF16),
            scratch(F32), scratch(F32), scratch(BF16), scratch(BF16),
        ],
        compiler_params=params(),
        cost_estimate=cost(27 * 2 * tokens * width * width, tokens * width * 20 + 18 * width * width * 2),
        name="mlp",
    )(embed, mixed, cotangent, live, small, shift, colwise, colwise, rowwise)


def embed_back_kernel(
    dproj_ref, norm_ref, qkv_ref, embed_ref, ghid_ref, pos_ref, small_ref,
    gemb_ref, gqkv_ref, gpos_ref, sums_ref, gnorm,
):
    step = pl.program_id(0)
    tokens = embed_ref.shape[0]
    weight = square(qkv_ref)

    @pl.when(step == 0)
    def _():
        sums_ref[...] = jnp.zeros_like(sums_ref)

        def body(rows):
            gnorm[rows, :] = nt(dproj_ref[0, rows, :], weight)

        row_tiles(tokens, body)

    @pl.when(step > 0)
    def _():
        def body(rows):
            gnorm[rows, :] += nt(dproj_ref[0, rows, :], weight)

        row_tiles(tokens, body)

    gqkv_ref[...] = tn(norm_ref[...], dproj_ref[0]).astype(BF16).reshape(gqkv_ref.shape)
    column = jnp.sum(dproj_ref[0].astype(F32), axis=0, keepdims=True)

    @pl.when(step == 0)
    def _():
        sums_ref[2:3, :] = column

    @pl.when(step == 2)
    def _():
        sums_ref[3:4, :] = column

        def body(rows):
            xhat, rstd = norm_parts(embed_ref[rows, :])
            grad = gnorm[rows, :]
            gemb = (ghid_ref[rows, :] + norm_back(xhat, rstd, grad, small_ref[7:8, :])).astype(BF16)
            gemb_ref[rows, :] = gemb
            sums_ref[0:1, :] += jnp.sum(gemb.astype(F32), axis=0, keepdims=True)
            sums_ref[1:2, :] += jnp.sum(grad, axis=0, keepdims=True)
            sums_ref[7:8, :] += jnp.sum(grad * xhat, axis=0, keepdims=True)

        row_tiles(tokens, body)
        gpos_ref[...] = tn(pos_ref[...], gemb_ref[...])


def embed_back(dproj, normed1, colwise, embed, g_hidden, pos_rows, small):
    tokens, width = embed.shape
    bands, deep = colwise.shape[1], colwise.shape[3]
    fixed = pl.BlockSpec((tokens, width), lambda s: (0, 0))
    whole = lambda a: pl.BlockSpec(a.shape, lambda s: (0, 0))
    return pl.pallas_call(
        embed_back_kernel,
        grid=(3,),
        in_specs=[
            pl.BlockSpec((1, tokens, width), lambda s: (s, 0, 0)), fixed,
            pl.BlockSpec((1, bands, 1, deep, width), lambda s: (1, 0, s, 0, 0)),
            fixed, fixed, whole(pos_rows), whole(small),
        ],
        out_specs=[
            fixed, pl.BlockSpec((bands, 1, deep, width), lambda s: (0, s, 0, 0)),
            pl.BlockSpec((128, width), lambda s: (0, 0)), pl.BlockSpec((16, width), lambda s: (0, 0)),
        ],
        out_shape=[
            jax.ShapeDtypeStruct((tokens, width), BF16),
            jax.ShapeDtypeStruct((bands, 3, deep, width), BF16),
            jax.ShapeDtypeStruct((128, width), F32),
            jax.ShapeDtypeStruct((16, width), F32),
        ],
        scratch_shapes=[pltpu.VMEM((tokens, width), F32)],
        compiler_params=params(),
        cost_estimate=cost(6 * 2 * tokens * width * width, tokens * width * 18 + 6 * width * width * 2),
        name="embed_back",
    )(dproj, normed1, colwise, embed, g_hidden, pos_rows, small)


def patch_grad_kernel(res_ref, g_ref, out_ref):
    out_ref[0] = tn(res_ref[...], g_ref[...]).astype(BF16)


def patch_grad(resized, g_emb):
    tokens, width = g_emb.shape
    return pl.pallas_call(
        patch_grad_kernel,
        grid=(4,),
        in_specs=[pl.BlockSpec((tokens, width), lambda s: (0, s)), pl.BlockSpec((tokens, width), lambda s: (0, 0))],
        out_specs=pl.BlockSpec((1, width, width), lambda s: (s, 0, 0)),
        out_shape=jax.ShapeDtypeStruct((4, width, width), BF16),
        compiler_params=params(),
        cost_estimate=cost(4 * 2 * tokens * width * width, tokens * width * 10 + 4 * width * width * 2),
        name="patch_grad",
    )(resized, g_emb)


def local(reps, owners, *arrays):
    (
        pixels, image_class, resize_a, resize_b, resize_c, posmap_a, posmap_b, posmap_c, cotangent,
        patch_kernel, pos_table, qkv_weight, out_weight, up_weight, down_weight, biases, up_bias, gains,
    ) = arrays
    tokens = pixels.shape[0]
    width = out_weight.shape[1]
    depth = out_weight.shape[0]
    shard = patch_kernel.shape[0]
    cells = pos_table.shape[0]
    slots = image_class.shape[1]

    def stacked(shards):
        return jnp.concatenate([w.reshape(depth, -1, width).transpose(1, 0, 2) for w in shards]).reshape(shard, width)

    small_here = jnp.concatenate([biases, gains, pos_table, up_bias.reshape(-1, depth)])
    bundle = jnp.concatenate(
        [patch_kernel, stacked([qkv_weight, out_weight]), stacked([up_weight]), down_weight]
    )
    share = 4 * shard // reps
    here = lax.dynamic_slice(bundle, (lax.axis_index("rep") * share, 0), (share, width))
    groups = lax.all_gather(here, ("rep", "fsdp"), axis=0, tiled=True)
    small_all = lax.all_gather(small_here, "fsdp", axis=0, tiled=False)
    groups = (
        groups.reshape(4, reps // 4, owners, share, width).transpose(0, 2, 1, 3, 4).reshape(4, owners, shard, width)
    )
    rowwise = groups.reshape(4, 4, width, width)
    colwise = groups.reshape(4, owners, 4, depth, width)
    if depth % 16 != 0:
        colwise = colwise.transpose(0, 2, 1, 3, 4).reshape(4, 1, 4, width, width)
    rows_of = small_all[:, : 9 + cells].transpose(1, 0, 2).reshape(9 + cells, width)
    small = jnp.pad(rows_of[:9].astype(F32), ((0, 7), (0, 0)))
    table = jnp.pad(rows_of[9:], ((0, 128 - cells), (0, 0)))
    shift = small_all[:, 9 + cells :].reshape(4, 1, width).astype(F32)

    segment, category, offset, live_rows = token_layout(image_class[0], tokens)
    live = live_rows[:, None].astype(F32)
    lists = chunk_lists(category)
    dense = (image_class[0, :1] == 0).astype(jnp.int32)
    lane = jnp.arange(128, dtype=jnp.int32)[None, :]
    same = segment[:, None] == lane
    onehot = same.astype(BF16)
    keymask = jnp.where(
        lane <= slots, jnp.where(same, 0.0, NEG), jnp.where((lane >= 64) & (lane < 67), -1.0, 0.0)
    ).astype(BF16)
    maps = jnp.concatenate([posmap_a, posmap_b, posmap_c, jnp.zeros((1, cells), BF16)])
    maps = jnp.pad(maps, ((0, 0), (0, 128 - cells)))
    first = jnp.array([0, GRID_A * GRID_A, GRID_A * GRID_A + GRID_B * GRID_B], jnp.int32)
    at = jnp.where(category < 3, first[jnp.minimum(category, 2)] + offset, maps.shape[0] - 1)
    pos_rows = jnp.take(maps, at, axis=0)
    cats = category[:, None]
    ra = jnp.pad(resize_a, ((0, -resize_a.shape[0] % 128), (0, 0)))
    rb = jnp.pad(resize_b, ((0, -resize_b.shape[0] % 128), (0, 0)))

    resized = resize(lists, pixels, cats, ra, rb, resize_c)
    embed, normed1, projected = embed_call(resized, rowwise, colwise, pos_rows, table, small)
    mixed, lse = attend(dense, projected, onehot, keymask)
    output, g_hidden, g_mixed, g_down, g_up, g_out, sums_mlp, g_shift = mlp_call(
        embed, mixed, cotangent, live, small, shift, rowwise, colwise
    )
    dproj = attend_back(dense, projected, g_mixed, mixed, lse, onehot, keymask)
    g_emb, g_qkv, g_pos, sums_embed = embed_back(dproj, normed1, colwise, embed, g_hidden, pos_rows, small)
    g_kernel = patch_grad(resized, g_emb)
    grad_pixels = unresize(lists, g_emb, groups, cats, ra, rb, resize_c, pixels.shape[1] // 3)

    def bands_of(blocks, number):
        if blocks.shape[0] != owners:
            blocks = blocks.reshape(number, owners, depth, width).transpose(1, 0, 2, 3)
        return blocks.reshape(owners, number * depth, width)

    g_small = jnp.concatenate([(sums_mlp + sums_embed)[:9], g_pos[:cells]]).reshape(9 + cells, owners, depth)
    g_small = jnp.concatenate(
        [g_small.transpose(1, 0, 2), g_shift.reshape(owners, -1, depth)], axis=1
    ).astype(BF16)
    scatter = lambda x: lax.psum_scatter(x, "fsdp", scatter_dimension=0, tiled=False)
    pieces = [
        scatter(g_kernel.reshape(owners, shard, width)),
        scatter(bands_of(g_qkv, 3)),
        scatter(bands_of(g_out, 1)),
        scatter(bands_of(g_up, 4)),
        scatter(g_down.reshape(owners, shard, width)),
        scatter(g_small),
    ]
    pieces = [lax.psum(p, "rep").astype(F32) for p in pieces]
    s_kernel, s_qkv, s_out, s_up, s_down, s_small = pieces
    unstack = lambda p: p.reshape(-1, depth, width).transpose(1, 0, 2).reshape(depth, -1)
    return (
        output, grad_pixels, s_kernel, s_small[9 : 9 + cells], unstack(s_qkv), s_out, unstack(s_up), s_down,
        s_small[:7], s_small[9 + cells :].reshape(-1), s_small[7:9],
    )


def solution(mesh):
    tokens = P(("rep", "fsdp"), None)
    rows, columns = P("fsdp", None), P(None, "fsdp")
    in_specs = (
        tokens, tokens, P(), P(), P(), P(), P(), P(), tokens,
        rows, columns, rows, rows, rows, rows, columns, P("fsdp"), columns,
    )
    out_specs = (tokens, tokens, rows, columns, rows, rows, rows, rows, columns, P("fsdp"), columns)
    reps, owners = mesh.shape["rep"], mesh.shape["fsdp"]

    def here(*arrays):
        return local(reps, owners, *arrays)

    return jax.shard_map(here, mesh=mesh, in_specs=in_specs, out_specs=out_specs, check_vma=False)
```

```python
import jax
import jax.numpy as jnp
from jax import lax
from jax.experimental import pallas as pl
from jax.experimental.pallas import tpu as pltpu
from jax.sharding import PartitionSpec as P

HEADS = 12
GRID_A = 30
GRID_B = 10
GRID_C = 5
CHUNK = 16
TILE = 256
F32 = jnp.float32
BF16 = jnp.bfloat16
NEG = -1e30
VMEM = 60 * 1024 * 1024


def nt(a, b):
    return lax.dot_general(a, b, (((1,), (1,)), ((), ())), preferred_element_type=F32)


def nn(a, b):
    return lax.dot_general(a, b, (((1,), (0,)), ((), ())), preferred_element_type=F32)


def tn(a, b):
    return lax.dot_general(a, b, (((0,), (0,)), ((), ())), preferred_element_type=F32)


def params(**more):
    return pltpu.CompilerParams(vmem_limit_bytes=VMEM, **more)


def cost(flops, moved, exps=0):
    return pl.CostEstimate(flops=int(flops), bytes_accessed=int(moved), transcendentals=int(exps))


def token_layout(classes, tokens_here):
    class_tokens = jnp.array(
        [GRID_A * GRID_A, GRID_B * GRID_B, GRID_C * GRID_C, 0], dtype=jnp.int32
    )
    class_ids = jnp.arange(4, dtype=jnp.int32)
    image_tokens = jnp.sum(
        jnp.where(classes[:, None] == class_ids[None, :], class_tokens[None, :], 0), axis=1
    )
    image_ends = jnp.cumsum(image_tokens)
    image_starts = image_ends - image_tokens
    positions = jnp.arange(tokens_here, dtype=jnp.int32)
    segment = jnp.sum((image_ends[None, :] <= positions[:, None]).astype(jnp.int32), axis=1)
    membership = segment[:, None] == jnp.arange(classes.shape[0], dtype=jnp.int32)[None, :]
    live_rows = jnp.any(membership, axis=1)
    category = jnp.sum(jnp.where(membership, classes[None, :], 0), axis=1) + jnp.where(
        live_rows, 0, 3
    )
    offset = positions - jnp.sum(jnp.where(membership, image_starts[None, :], 0), axis=1)
    return (segment, category, offset, live_rows)


def chunk_lists(category):
    chunks = category.reshape(-1, CHUNK)
    here = jnp.any(chunks[None, :, :] == jnp.arange(3, dtype=jnp.int32)[:, None, None], axis=2)
    place = jnp.cumsum(here.astype(jnp.int32), axis=1) - 1
    count = chunks.shape[0]
    ids = jnp.arange(count, dtype=jnp.int32)
    hit = here[:, :, None] & (place[:, :, None] == ids[None, None, :])
    listed = jnp.sum(jnp.where(hit, ids[None, :, None], 0), axis=1)
    return jnp.concatenate([place[:, -1:] + 1, listed], axis=1).astype(jnp.int32)


def resize_rows(lists, cat_ref, src_ref, out_ref, lhs, class_id, width, product, columns):
    number = lists[class_id, 0]

    @pl.loop(0, (number + TILE // CHUNK - 1) // (TILE // CHUNK))
    def _(t):
        base = t * (TILE // CHUNK)
        for u in range(TILE // CHUNK):
            row = pl.multiple_of(lists[class_id, 1 + jnp.minimum(base + u, number - 1)] * CHUNK, CHUNK)
            lhs[u * CHUNK : (u + 1) * CHUNK, 0:width] = src_ref[pl.ds(row, CHUNK), 0:width]
        total = product(lhs[:, 0:width])
        for u in range(TILE // CHUNK):

            @pl.when(base + u < number)
            def _():
                row = pl.multiple_of(lists[class_id, 1 + base + u] * CHUNK, CHUNK)
                mine = cat_ref[pl.ds(row, CHUNK), :] == class_id
                old = out_ref[pl.ds(row, CHUNK), 0:columns].astype(F32)
                new = total[u * CHUNK : (u + 1) * CHUNK, :]
                out_ref[pl.ds(row, CHUNK), 0:columns] = jnp.where(mine, new, old).astype(
                    out_ref.dtype
                )


def resize_kernel(lists, px_ref, cat_ref, ra_ref, rb_ref, rc_ref, out_ref, lhs):
    out_ref[...] = jnp.zeros_like(out_ref)
    for class_id, matrix in enumerate((ra_ref, rb_ref, rc_ref)):
        resize_rows(
            lists, cat_ref, px_ref, out_ref, lhs, class_id, matrix.shape[0],
            lambda rows, matrix=matrix: nn(rows, matrix[...]), matrix.shape[1],
        )


def resize(lists, pixels, category, ra, rb, rc):
    tokens, wide = pixels.shape
    area = wide // 3
    base = rc.shape[1]
    whole = lambda a: pl.BlockSpec(a.shape, lambda c, s: (0, 0))
    return pl.pallas_call(
        resize_kernel,
        grid_spec=pltpu.PrefetchScalarGridSpec(
            num_scalar_prefetch=1,
            grid=(3,),
            in_specs=[pl.BlockSpec((tokens, area), lambda c, s: (0, c)), whole(category), whole(ra), whole(rb), whole(rc)],
            out_specs=pl.BlockSpec((tokens, base), lambda c, s: (0, c)),
            scratch_shapes=[pltpu.VMEM((TILE, area), BF16)],
        ),
        out_shape=jax.ShapeDtypeStruct((tokens, 3 * base), BF16),
        compiler_params=params(),
        cost_estimate=cost(tokens * 3 * base * 1200 * 2, tokens * wide * 2 + tokens * base * 6),
        name="resize",
    )(lists, pixels, category, ra, rb, rc)


def unresize_kernel(lists, g_ref, w_ref, cat_ref, ra_ref, rb_ref, rc_ref, *rest):
    out_ref, grow, lhs = rest[-3:]
    out_ref[...] = jnp.zeros_like(out_ref)
    grow[...] = nt(g_ref[...], w_ref[0, 0]).astype(BF16)
    for class_id, matrix in enumerate((ra_ref, rb_ref, rc_ref)):
        resize_rows(
            lists, cat_ref, grow, out_ref, lhs, class_id, grow.shape[1],
            lambda rows, matrix=matrix: nt(rows, matrix[...]), matrix.shape[0],
        )


def unresize(lists, g_emb, groups, category, ra, rb, rc, area, channel, part, parts, before):
    tokens, width = g_emb.shape
    base = rc.shape[1]
    rows = tokens // parts
    whole = lambda a: pl.BlockSpec(a.shape, lambda c, s: (0, 0))
    some = lambda a: pl.BlockSpec((rows, a.shape[1]), lambda c, s: (part, 0))
    kernels = groups.reshape(4, 3, base, width)
    more = [] if before is None else [before]
    return pl.pallas_call(
        unresize_kernel,
        grid_spec=pltpu.PrefetchScalarGridSpec(
            num_scalar_prefetch=1,
            grid=(1,),
            in_specs=[
                some(g_emb), pl.BlockSpec((1, 1, base, width), lambda c, s: (0, channel, 0, 0)),
                some(category), whole(ra), whole(rb), whole(rc),
            ] + [pl.BlockSpec(memory_space=pl.ANY)] * len(more),
            out_specs=pl.BlockSpec((rows, area), lambda c, s: (part, channel)),
            scratch_shapes=[pltpu.VMEM((rows, base), BF16), pltpu.VMEM((TILE, base), BF16)],
        ),
        out_shape=jax.ShapeDtypeStruct((tokens, 3 * area), BF16),
        input_output_aliases={7: 0} if more else {},
        compiler_params=params(),
        cost_estimate=cost(1e6, 1e5),
        name="unresize",
    )(lists, g_emb, kernels, category, ra, rb, rc, *more)


def norm_parts(values):
    center = values - jnp.mean(values, axis=-1, keepdims=True)
    rstd = lax.rsqrt(jnp.mean(center * center, axis=-1, keepdims=True) + 1e-06)
    return center * rstd, rstd


def norm_back(xhat, rstd, grad, gain):
    dxhat = grad * gain
    return rstd * (
        dxhat
        - jnp.mean(dxhat, axis=-1, keepdims=True)
        - xhat * jnp.mean(dxhat * xhat, axis=-1, keepdims=True)
    )


def square(ref):
    value = ref[...]
    return value.reshape(-1, value.shape[-1])


def row_tiles(tokens, body):
    body(pl.ds(0, tokens))


def embed_kernel(res_ref, kern_ref, qkv_ref, pos_ref, table_ref, small_ref, embed_ref, norm_ref, proj_ref):
    step = pl.program_id(0)
    tokens = res_ref.shape[0]

    @pl.when(step == 0)
    def _():
        def body(rows):
            embed_ref[rows, :] = (
                nn(res_ref[rows, :], square(kern_ref)) + small_ref[0:1, :] + nn(pos_ref[rows, :], table_ref[...])
            )

        row_tiles(tokens, body)

    @pl.when((step > 0) & (step < 4))
    def _():
        def body(rows):
            embed_ref[rows, :] += nn(res_ref[rows, :], square(kern_ref))

        row_tiles(tokens, body)

    @pl.when(step == 3)
    def _():
        def body(rows):
            xhat, _ = norm_parts(embed_ref[rows, :])
            norm_ref[rows, :] = (xhat * small_ref[7:8, :] + small_ref[1:2, :]).astype(BF16)

        row_tiles(tokens, body)

    @pl.when(step >= 4)
    def _():
        shift = jnp.where(
            step == 4, small_ref[2:3, :], jnp.where(step == 6, small_ref[3:4, :], jnp.zeros_like(small_ref[3:4, :]))
        )

        def body(rows):
            proj_ref[rows, :] = (nn(norm_ref[rows, :], square(qkv_ref)) + shift).astype(BF16)

        row_tiles(tokens, body)


def embed_call(resized, rowwise, colwise, pos_rows, table, small):
    tokens = resized.shape[0]
    width = small.shape[1]
    bands, deep = colwise.shape[1], colwise.shape[3]
    whole = lambda a: pl.BlockSpec(a.shape, lambda s: (0, 0))
    fixed = pl.BlockSpec((tokens, width), lambda s: (0, 0))
    return pl.pallas_call(
        embed_kernel,
        grid=(7,),
        in_specs=[
            pl.BlockSpec((tokens, width), lambda s: (0, jnp.minimum(s, 3))),
            pl.BlockSpec((1, 1, width, width), lambda s: (0, jnp.minimum(s, 3), 0, 0)),
            pl.BlockSpec((1, bands, 1, deep, width), lambda s: (1, 0, jnp.maximum(s - 4, 0), 0, 0)),
            whole(pos_rows), whole(table), whole(small),
        ],
        out_specs=[fixed, fixed, pl.BlockSpec((tokens, width), lambda s: (0, jnp.maximum(s - 4, 0)))],
        out_shape=[
            jax.ShapeDtypeStruct((tokens, width), F32),
            jax.ShapeDtypeStruct((tokens, width), BF16),
            jax.ShapeDtypeStruct((tokens, 3 * width), BF16),
        ],
        compiler_params=params(),
        cost_estimate=cost(7 * 2 * tokens * width * width, tokens * width * 20 + 7 * width * width * 2),
        name="embed",
    )(resized, rowwise, colwise, pos_rows, table, small)


def attend_kernel(dense_ref, q_ref, k_ref, v_ref, oh_ref, km_ref, o_ref, lse_ref, kaug, vaug):
    tokens = q_ref.shape[0]
    lane = lax.broadcasted_iota(jnp.int32, (1, 128), 1)
    kaug[:, 0:128] = k_ref[...]
    kaug[:, 128:256] = km_ref[...]
    vaug[:, 0:128] = v_ref[...]
    vaug[:, 128:256] = jnp.ones((tokens, 128), BF16)

    def tile(rows, cols):
        q = q_ref[rows, :] * jnp.asarray(0.125, BF16)
        oh = oh_ref[rows, :]
        keys, vals = kaug[cols, :], vaug[cols, :]
        outs, logs = [], []
        for h in range(2):
            mine = (lane < 64) if h == 0 else (lane >= 64)
            left = jnp.concatenate([jnp.where(mine, q, jnp.zeros_like(q)), oh], axis=1)
            scores = nt(left, keys)
            top = jnp.max(scores, axis=1, keepdims=True)
            weights = jnp.exp(scores - top).astype(BF16)
            both = nn(weights, vals)
            total = both[:, 128:256]
            outs.append(both[:, 0:128] / total)
            logs.append(top + jnp.log(total))
        o_ref[rows, :] = jnp.where(lane < 64, outs[0], outs[1]).astype(o_ref.dtype)
        lse_ref[rows, :] = jnp.where(lane < 64, logs[0], logs[1])

    attend_tiles(dense_ref, tokens, tile)


def attend_tiles(dense_ref, tokens, tile):
    @pl.when(dense_ref[0] != 0)
    def _():
        @pl.loop(0, tokens // TILE)
        def _(t):
            tile(pl.ds(pl.multiple_of(t * TILE, TILE), TILE), pl.ds(0, tokens))

    @pl.when(dense_ref[0] == 0)
    def _():
        @pl.loop(0, tokens // TILE)
        def _(t):
            first = pl.multiple_of(jnp.clip(t * TILE - 128, 0, tokens - 512), 128)
            tile(pl.ds(pl.multiple_of(t * TILE, TILE), TILE), pl.ds(first, 512))


def attend(dense, projected, onehot, keymask):
    tokens = projected.shape[0]
    pairs = projected.shape[1] // 3 // 128
    part = lambda at: pl.BlockSpec((tokens, 128), lambda j, d: (0, at + j))
    whole = pl.BlockSpec((tokens, 128), lambda j, d: (0, 0))
    return pl.pallas_call(
        attend_kernel,
        grid_spec=pltpu.PrefetchScalarGridSpec(
            num_scalar_prefetch=1,
            grid=(pairs,),
            in_specs=[part(0), part(pairs), part(2 * pairs), whole, whole],
            out_specs=[part(0), part(0)],
            scratch_shapes=[pltpu.VMEM((tokens, 256), BF16), pltpu.VMEM((tokens, 256), BF16)],
        ),
        out_shape=[
            jax.ShapeDtypeStruct((tokens, pairs * 128), BF16),
            jax.ShapeDtypeStruct((tokens, pairs * 128), F32),
        ],
        compiler_params=params(),
        cost_estimate=cost(2 * 2 * 12 * tokens * tokens * 256, tokens * 2304 * 2 + tokens * 768 * 6, 12 * tokens * tokens),
        name="attend",
    )(dense, projected, projected, projected, onehot, keymask)


def split3(x):
    high = x.astype(BF16)
    rest = x - high.astype(F32)
    middle = rest.astype(BF16)
    low = (rest - middle.astype(F32)).astype(BF16)
    return high, middle, low


def attend_back_kernel(
    dense_ref, q_ref, k_ref, v_ref, g_ref, o_ref, lse_ref, oh_ref, km_ref, out_ref, kaug, vaug, dkeys, dvals
):
    tokens = q_ref.shape[0]
    lane = lax.broadcasted_iota(jnp.int32, (1, 128), 1)
    kaug[:, 0:128] = k_ref[...]
    kaug[:, 128:256] = km_ref[...]
    vaug[:, 0:128] = v_ref[...]
    vaug[:, 128:256] = jnp.broadcast_to(jnp.where(lane < 3, -1.0, 0.0).astype(BF16), (tokens, 128))
    dkeys[...] = jnp.zeros_like(dkeys)
    dvals[...] = jnp.zeros_like(dvals)

    def put(parts, at, other):
        for i, piece in enumerate(parts):
            other = jnp.where(lane == at + i, piece, other)
        return other

    def tile(rows, cols):
        q = q_ref[rows, :] * jnp.asarray(0.125, BF16)
        g = g_ref[rows, :]
        oh = oh_ref[rows, :]
        go = g.astype(F32) * o_ref[rows, :].astype(F32)
        lse = lse_ref[rows, :]
        keys, vals = kaug[cols, :], vaug[cols, :]
        plain = keys[:, 0:128]
        dqs, dkt, dvt = [], None, None
        for h in range(2):
            mine = (lane < 64) if h == 0 else (lane >= 64)
            delta = jnp.sum(jnp.where(mine, go, 0.0), axis=1, keepdims=True)
            qm = jnp.where(mine, q, jnp.zeros_like(q))
            gm = jnp.where(mine, g, jnp.zeros_like(g))
            qa = jnp.concatenate([qm, put(split3(lse[:, 64 * h : 64 * h + 1]), 64, oh)], axis=1)
            ga = jnp.concatenate([gm, put(split3(delta), 0, jnp.zeros_like(oh))], axis=1)
            probs = jnp.exp(nt(keys, qa))
            dscores = (probs * nt(vals, ga)).astype(BF16)
            a, b = nn(probs.astype(BF16), gm), nn(dscores, qm)
            dvt = a if dvt is None else dvt + a
            dkt = b if dkt is None else dkt + b
            dqs.append(tn(dscores, plain))
        out_ref[0, rows, :] = (jnp.where(lane < 64, dqs[0], dqs[1]) * 0.125).astype(BF16)
        dkeys[cols, :] += dkt
        dvals[cols, :] += dvt

    attend_tiles(dense_ref, tokens, tile)
    out_ref[1] = dkeys[...].astype(BF16)
    out_ref[2] = dvals[...].astype(BF16)


def attend_back(dense, projected, g_mixed, mixed, lse, onehot, keymask, start, number):
    tokens = projected.shape[0]
    pairs = projected.shape[1] // 3 // 128
    part = lambda at: pl.BlockSpec((tokens, 128), lambda j, d: (0, at + start + j))
    whole = pl.BlockSpec((tokens, 128), lambda j, d: (0, 0))
    return pl.pallas_call(
        attend_back_kernel,
        grid_spec=pltpu.PrefetchScalarGridSpec(
            num_scalar_prefetch=1,
            grid=(number,),
            in_specs=[part(0), part(pairs), part(2 * pairs), part(0), part(0), part(0), whole, whole],
            out_specs=pl.BlockSpec((3, tokens, 128), lambda j, d: (0, 0, j)),
            scratch_shapes=[
                pltpu.VMEM((tokens, 256), BF16), pltpu.VMEM((tokens, 256), BF16),
                pltpu.VMEM((tokens, 128), F32), pltpu.VMEM((tokens, 128), F32),
            ],
        ),
        out_shape=jax.ShapeDtypeStruct((3, tokens, number * 128), BF16),
        compiler_params=params(),
        cost_estimate=cost(5 * 2 * 2 * number * tokens * tokens * 256, tokens * 128 * number * 22, 2 * number * tokens * tokens),
        name="attend_back",
    )(dense, projected, projected, projected, g_mixed, mixed, lse, onehot, keymask)


def mlp_kernel(
    embed_ref, mixed_ref, cot_ref, live_ref, small_ref, shift_ref, wo_ref, up_ref, down_ref,
    out_ref, ghid_ref, gmixed_ref, gdown_ref, gup_ref, gwo_ref, sums_ref, gshift_ref,
    hidden, xhats, norm2, gbranch, total, gnorm, act, gpre,
):
    step = pl.program_id(0)
    tokens = embed_ref.shape[0]

    @pl.when(step == 0)
    def _():
        def body(rows):
            value = embed_ref[rows, :] + nn(mixed_ref[rows, :], square(wo_ref)) + small_ref[4:5, :]
            hidden[rows, :] = value
            total[rows, :] = value + small_ref[6:7, :]
            xhat, _ = norm_parts(value)
            norm2[rows, :] = (xhat * small_ref[8:9, :] + small_ref[5:6, :]).astype(BF16)
            gbranch[rows, :] = (cot_ref[rows, :].astype(F32) * live_ref[rows, :]).astype(BF16)
            gnorm[rows, :] = jnp.zeros_like(value)

        row_tiles(tokens, body)

    up, down = square(up_ref), square(down_ref)

    def body(rows):
        x = nn(norm2[rows, :], up) + shift_ref[0]
        square_x = x * x
        t = jnp.tanh(0.7978845608028654 * (x + 0.044715 * (square_x * x)))
        half = 0.5 * (1.0 + t)
        acts = (x * half).astype(BF16)
        act[rows, :] = acts
        total[rows, :] += nn(acts, down)
        slope = half + 0.5 * x * (1.0 - t * t) * (
            0.7978845608028654 + (0.7978845608028654 * 3 * 0.044715) * square_x
        )
        gp = (nt(gbranch[rows, :], down) * slope).astype(BF16)
        gpre[rows, :] = gp
        gnorm[rows, :] += nt(gp, up)

    row_tiles(tokens, body)
    gdown_ref[0] = tn(act[...], gbranch[...]).astype(BF16)
    gup_ref[...] = tn(norm2[...], gpre[...]).astype(BF16).reshape(gup_ref.shape)
    gshift_ref[0] = jnp.sum(gpre[...].astype(F32), axis=0, keepdims=True)

    @pl.when(step == 3)
    def _():
        sums_ref[...] = jnp.zeros_like(sums_ref)
        wo = square(wo_ref)

        def body(rows):
            out_ref[rows, :] = (total[rows, :] * live_ref[rows, :]).astype(BF16)
            xhat, rstd = norm_parts(hidden[rows, :])
            grad = gnorm[rows, :]
            gout = gbranch[rows, :].astype(F32)
            ghid = gout + norm_back(xhat, rstd, grad, small_ref[8:9, :])
            ghid_ref[rows, :] = ghid
            gmix = ghid.astype(BF16)
            xhats[rows, :] = gmix
            gmixed_ref[rows, :] = nt(gmix, wo).astype(BF16)
            sums_ref[4:5, :] += jnp.sum(gmix.astype(F32), axis=0, keepdims=True)
            sums_ref[5:6, :] += jnp.sum(grad, axis=0, keepdims=True)
            sums_ref[6:7, :] += jnp.sum(gout, axis=0, keepdims=True)
            sums_ref[8:9, :] += jnp.sum(grad * xhat, axis=0, keepdims=True)

        row_tiles(tokens, body)
        gwo_ref[...] = tn(mixed_ref[...], xhats[...]).astype(BF16).reshape(gwo_ref.shape)


def mlp_call(embed, mixed, cotangent, live, small, shift, rowwise, colwise):
    tokens, width = embed.shape
    bands, deep = colwise.shape[1], colwise.shape[3]
    fixed = pl.BlockSpec((tokens, width), lambda s: (0, 0))
    whole = lambda a: pl.BlockSpec(a.shape, lambda s: (0, 0))
    band = lambda group, at: pl.BlockSpec((1, bands, 1, deep, width), lambda s: (group, 0, at(s), 0, 0))
    scratch = lambda kind: pltpu.VMEM((tokens, width), kind)
    return pl.pallas_call(
        mlp_kernel,
        grid=(4,),
        in_specs=[
            fixed, fixed, fixed, whole(live), whole(small),
            pl.BlockSpec((1, 1, width), lambda s: (s, 0, 0)),
            band(1, lambda s: 3), band(2, lambda s: s),
            pl.BlockSpec((1, 1, width, width), lambda s: (3, s, 0, 0)),
        ],
        out_specs=[
            fixed, fixed, fixed,
            pl.BlockSpec((1, width, width), lambda s: (s, 0, 0)),
            pl.BlockSpec((bands, 1, deep, width), lambda s: (0, s, 0, 0)),
            pl.BlockSpec((bands, deep, width), lambda s: (0, 0, 0)),
            pl.BlockSpec((16, width), lambda s: (0, 0)),
            pl.BlockSpec((1, 1, width), lambda s: (s, 0, 0)),
        ],
        out_shape=[
            jax.ShapeDtypeStruct((tokens, width), BF16),
            jax.ShapeDtypeStruct((tokens, width), F32),
            jax.ShapeDtypeStruct((tokens, width), BF16),
            jax.ShapeDtypeStruct((4, width, width), BF16),
            jax.ShapeDtypeStruct((bands, 4, deep, width), BF16),
            jax.ShapeDtypeStruct((bands, deep, width), BF16),
            jax.ShapeDtypeStruct((16, width), F32),
            jax.ShapeDtypeStruct((4, 1, width), F32),
        ],
        scratch_shapes=[
            scratch(F32), scratch(BF16), scratch(BF16), scratch(BF16),
            scratch(F32), scratch(F32), scratch(BF16), scratch(BF16),
        ],
        compiler_params=params(),
        cost_estimate=cost(27 * 2 * tokens * width * width, tokens * width * 20 + 18 * width * width * 2),
        name="mlp",
    )(embed, mixed, cotangent, live, small, shift, colwise, colwise, rowwise)


def store_split(core, value, mine_ref, other_ref):
    shape = mine_ref.shape
    pairs = value.reshape(-1, 2, shape[-2], shape[-1])
    first, second = pairs[:, 0].reshape(shape), pairs[:, 1].reshape(shape)

    @pl.when(core == 0)
    def _():
        mine_ref[...] = first
        other_ref[...] = second

    @pl.when(core != 0)
    def _():
        mine_ref[...] = second
        other_ref[...] = first


def qkv_grad_kernel(core_ref, norm_ref, dproj_ref, gwo_ref, mine_ref, other_ref):
    step = pl.program_id(0)

    @pl.when(step < 3)
    def _():
        value = tn(norm_ref[...], dproj_ref[0]).astype(BF16)
        store_split(core_ref[0], value, mine_ref, other_ref)

    @pl.when(step == 3)
    def _():
        store_split(core_ref[0], square(gwo_ref), mine_ref, other_ref)


def qkv_grad(core, normed1, dproj, g_out):
    tokens, width = normed1.shape
    bands, deep = g_out.shape[0], g_out.shape[1]
    half = (bands // 2, deep) if bands > 1 else (1, width // 2)
    pair = pl.BlockSpec((half[0], 1, half[1], width), lambda s, c: (0, s, 0, 0))
    shape = jax.ShapeDtypeStruct((half[0], 4, half[1], width), BF16)
    return pl.pallas_call(
        qkv_grad_kernel,
        grid_spec=pltpu.PrefetchScalarGridSpec(
            num_scalar_prefetch=1,
            grid=(4,),
            in_specs=[
                pl.BlockSpec((tokens, width), lambda s, c: (0, 0)),
                pl.BlockSpec((1, tokens, width), lambda s, c: (jnp.minimum(s, 2), 0, 0)),
                pl.BlockSpec(g_out.shape, lambda s, c: (0, 0, 0)),
            ],
            out_specs=[pair, pair],
        ),
        out_shape=[shape, shape],
        compiler_params=params(),
        cost_estimate=cost(1e6, 1e5),
        name="qkv_grad",
    )(core, normed1, dproj, g_out)


def embed_back_kernel(
    dproj_ref, qkv_ref, embed_ref, ghid_ref, pos_ref, small_ref, gemb_ref, gpos_ref, sums_ref, gnorm
):
    step = pl.program_id(0)
    tokens = embed_ref.shape[0]
    weight = square(qkv_ref)

    column = jnp.sum(dproj_ref[0].astype(F32), axis=0, keepdims=True)

    @pl.when(step == 0)
    def _():
        sums_ref[...] = jnp.zeros_like(sums_ref)
        sums_ref[2:3, :] = column

        def body(rows):
            gnorm[rows, :] = nt(dproj_ref[0, rows, :], weight)

        row_tiles(tokens, body)

    @pl.when(step == 1)
    def _():
        def body(rows):
            gnorm[rows, :] += nt(dproj_ref[0, rows, :], weight)

        row_tiles(tokens, body)

    @pl.when(step == 2)
    def _():
        sums_ref[3:4, :] = column

        def body(rows):
            grad = gnorm[rows, :] + nt(dproj_ref[0, rows, :], weight)
            xhat, rstd = norm_parts(embed_ref[rows, :])
            gemb = (ghid_ref[rows, :] + norm_back(xhat, rstd, grad, small_ref[7:8, :])).astype(BF16)
            gemb_ref[rows, :] = gemb
            sums_ref[0:1, :] += jnp.sum(gemb.astype(F32), axis=0, keepdims=True)
            sums_ref[1:2, :] += jnp.sum(grad, axis=0, keepdims=True)
            sums_ref[7:8, :] += jnp.sum(grad * xhat, axis=0, keepdims=True)

        row_tiles(tokens, body)
        gpos_ref[...] = tn(pos_ref[...], gemb_ref[...])


def embed_back(dproj, colwise, embed, g_hidden, pos_rows, small):
    tokens, width = embed.shape
    bands, deep = colwise.shape[1], colwise.shape[3]
    fixed = pl.BlockSpec((tokens, width), lambda s: (0, 0))
    whole = lambda a: pl.BlockSpec(a.shape, lambda s: (0, 0))
    return pl.pallas_call(
        embed_back_kernel,
        grid=(3,),
        in_specs=[
            pl.BlockSpec((1, tokens, width), lambda s: (s, 0, 0)),
            pl.BlockSpec((1, bands, 1, deep, width), lambda s: (1, 0, s, 0, 0)),
            fixed, fixed, whole(pos_rows), whole(small),
        ],
        out_specs=[
            fixed, pl.BlockSpec((128, width), lambda s: (0, 0)), pl.BlockSpec((16, width), lambda s: (0, 0)),
        ],
        out_shape=[
            jax.ShapeDtypeStruct((tokens, width), BF16),
            jax.ShapeDtypeStruct((128, width), F32),
            jax.ShapeDtypeStruct((16, width), F32),
        ],
        scratch_shapes=[pltpu.VMEM((tokens, width), F32)],
        compiler_params=params(),
        cost_estimate=cost(1e6, 1e5),
        name="embed_back",
    )(dproj, colwise, embed, g_hidden, pos_rows, small)


def patch_grad_kernel(core_ref, res_ref, g_ref, small_ref, mine_ref, other_ref):
    shard = mine_ref.shape[1] - small_ref.shape[1]
    value = tn(res_ref[...], g_ref[...]).astype(BF16).reshape(-1, 2, shard, mine_ref.shape[2])
    tail = small_ref[...].reshape(-1, 2, small_ref.shape[1], small_ref.shape[2])

    def store(ref, which):
        ref[:, 0:shard, :] = value[:, which]
        ref[:, shard:, :] = tail[:, which]

    @pl.when(core_ref[0] == 0)
    def _():
        store(mine_ref, 0)
        store(other_ref, 1)

    @pl.when(core_ref[0] != 0)
    def _():
        store(mine_ref, 1)
        store(other_ref, 0)


def patch_grad(core, resized, g_emb, g_small):
    tokens, width = g_emb.shape
    owners, packed = g_small.shape[0], g_small.shape[1]
    shard = 4 * width // owners
    pair = pl.BlockSpec((owners // 8, shard + packed, width), lambda s, c: (s, 0, 0))
    shape = jax.ShapeDtypeStruct((owners // 2, shard + packed, width), BF16)
    return pl.pallas_call(
        patch_grad_kernel,
        grid_spec=pltpu.PrefetchScalarGridSpec(
            num_scalar_prefetch=1,
            grid=(4,),
            in_specs=[
                pl.BlockSpec((tokens, width), lambda s, c: (0, s)),
                pl.BlockSpec((tokens, width), lambda s, c: (0, 0)),
                pl.BlockSpec((owners // 4, packed, width), lambda s, c: (s, 0, 0)),
            ],
            out_specs=[pair, pair],
        ),
        out_shape=[shape, shape],
        compiler_params=params(),
        cost_estimate=cost(1e6, 1e5),
        name="patch_grad",
    )(core, resized, g_emb, g_small)


def bit_of(axis, bit):
    return (lax.axis_index(axis) >> bit) & 1


class Sum:
    def __init__(self, mine, other, reps, owners, steps):
        self.sizes = dict(rep=reps, fsdp=owners)
        self.lead = [("fsdp", b) for b in range(1, owners.bit_length() - 1)][::-1]
        self.steps = [("fsdp", 0)] + steps
        self.back = [s for s in steps if s[0] == "rep"][::-1]
        shape = (2,) * len(self.lead) + mine.shape[1:]
        self.launch(mine.reshape(shape), other.reshape(shape))

    def launch(self, kept, sent):
        axis, bit = (self.steps or self.back)[0]
        pairs = [(i, i ^ (1 << bit)) for i in range(self.sizes[axis])]
        kept, sent = lax.optimization_barrier((kept, sent))
        self.kept, self.flying = kept, lax.ppermute(sent, axis, pairs)

    def land(self):
        if not self.steps and not self.back:
            return
        if self.steps:
            self.steps.pop(0)
            value = (self.kept.astype(F32) + self.flying.astype(F32)).astype(BF16)
        else:
            axis, bit = self.back.pop(0)
            low = bit_of(axis, bit) == 0
            a, b = self.kept, self.flying
            value = jnp.concatenate([jnp.where(low, a, b), jnp.where(low, b, a)])
        if self.steps:
            axis, bit = self.steps[0]
            if axis == "fsdp":
                at = self.lead.index((axis, bit))
                self.lead.remove((axis, bit))
            else:
                at = len(self.lead)
                value = value.reshape(value.shape[:at] + (2, value.shape[at] // 2) + value.shape[at + 1 :])
            mine = bit_of(axis, bit)
            pick = lambda i: lax.dynamic_index_in_dim(value, i, at, keepdims=False)
            self.launch(pick(mine), pick(1 - mine))
        elif self.back:
            self.launch(value, value)
        else:
            self.kept = value

    def total(self):
        while self.steps or self.back:
            self.land()
        return self.kept


def beside(sums, work, value):
    value = lax.optimization_barrier((value, *[one.kept for one in sums]))[0]
    value, *kept = lax.optimization_barrier((work(value), *[one.kept for one in sums]))
    for one, k in zip(sums, kept):
        one.kept = k
    return value


def local(reps, owners, *arrays):
    (
        pixels, image_class, resize_a, resize_b, resize_c, posmap_a, posmap_b, posmap_c, cotangent,
        patch_kernel, pos_table, qkv_weight, out_weight, up_weight, down_weight, biases, up_bias, gains,
    ) = arrays
    tokens = pixels.shape[0]
    width = out_weight.shape[1]
    depth = out_weight.shape[0]
    shard = patch_kernel.shape[0]
    cells = pos_table.shape[0]
    slots = image_class.shape[1]

    def stacked(shards):
        return jnp.concatenate([w.reshape(depth, -1, width).transpose(1, 0, 2) for w in shards]).reshape(shard, width)

    small_here = jnp.concatenate([biases, gains, pos_table, up_bias.reshape(-1, depth)])
    bundle = jnp.concatenate(
        [patch_kernel, stacked([qkv_weight, out_weight]), stacked([up_weight]), down_weight]
    )
    share = 4 * shard // reps
    here = lax.dynamic_slice(bundle, (lax.axis_index("rep") * share, 0), (share, width))
    groups = lax.all_gather(here, ("rep", "fsdp"), axis=0, tiled=True)
    small_all = lax.all_gather(small_here, "fsdp", axis=0, tiled=False)
    groups = (
        groups.reshape(4, reps // 4, owners, share, width).transpose(0, 2, 1, 3, 4).reshape(4, owners, shard, width)
    )
    rowwise = groups.reshape(4, 4, width, width)
    colwise = groups.reshape(4, owners, 4, depth, width)
    if depth % 16 != 0:
        colwise = colwise.transpose(0, 2, 1, 3, 4).reshape(4, 1, 4, width, width)
    rows_of = small_all[:, : 9 + cells].transpose(1, 0, 2).reshape(9 + cells, width)
    small = jnp.pad(rows_of[:9].astype(F32), ((0, 7), (0, 0)))
    table = jnp.pad(rows_of[9:], ((0, 128 - cells), (0, 0)))
    shift = small_all[:, 9 + cells :].reshape(4, 1, width).astype(F32)

    segment, category, offset, live_rows = token_layout(image_class[0], tokens)
    live = live_rows[:, None].astype(F32)
    lists = chunk_lists(category)
    dense = (image_class[0, :1] == 0).astype(jnp.int32)
    lane = jnp.arange(128, dtype=jnp.int32)[None, :]
    same = segment[:, None] == lane
    onehot = same.astype(BF16)
    keymask = jnp.where(
        lane <= slots, jnp.where(same, 0.0, NEG), jnp.where((lane >= 64) & (lane < 67), -1.0, 0.0)
    ).astype(BF16)
    maps = jnp.concatenate([posmap_a, posmap_b, posmap_c, jnp.zeros((1, cells), BF16)])
    maps = jnp.pad(maps, ((0, 0), (0, 128 - cells)))
    first = jnp.array([0, GRID_A * GRID_A, GRID_A * GRID_A + GRID_B * GRID_B], jnp.int32)
    at = jnp.where(category < 3, first[jnp.minimum(category, 2)] + offset, maps.shape[0] - 1)
    pos_rows = jnp.take(maps, at, axis=0)
    cats = category[:, None]
    ra = jnp.pad(resize_a, ((0, -resize_a.shape[0] % 128), (0, 0)))
    rb = jnp.pad(resize_b, ((0, -resize_b.shape[0] % 128), (0, 0)))

    resized = resize(lists, pixels, cats, ra, rb, resize_c)
    embed, normed1, projected = embed_call(resized, rowwise, colwise, pos_rows, table, small)
    mixed, lse = attend(dense, projected, onehot, keymask)
    output, g_hidden, g_mixed, g_down, g_up, g_out, sums_mlp, g_shift = mlp_call(
        embed, mixed, cotangent, live, small, shift, rowwise, colwise
    )
    def bands_of(blocks, number):
        if blocks.shape[0] != owners:
            blocks = blocks.reshape(number, owners, depth, width).transpose(1, 0, 2, 3)
        return blocks.reshape(owners, number * depth, width)

    scatter = lambda x: lax.psum_scatter(x, "fsdp", scatter_dimension=0, tiled=False)
    s_down = scatter(g_down.reshape(owners, shard, width))
    s_up = scatter(bands_of(g_up, 4))
    pairs = width // 128
    dproj = attend_back(dense, projected, g_mixed, mixed, lse, onehot, keymask, 0, pairs)
    dproj = lax.optimization_barrier((dproj, s_down))[0]
    core = bit_of("fsdp", 0).reshape(1)
    own, rep = owners.bit_length() - 1, reps.bit_length() - 1
    others = [("fsdp", b) for b in range(1, own)]
    over_reps = [("rep", b) for b in range(rep)]
    g_emb, g_pos, sums_embed = embed_back(dproj, colwise, embed, g_hidden, pos_rows, small)
    g_small = jnp.concatenate([(sums_mlp + sums_embed)[:9], g_pos[:cells]]).reshape(9 + cells, owners, depth)
    g_small = jnp.concatenate(
        [g_small.transpose(1, 0, 2), g_shift.reshape(owners, -1, depth)], axis=1
    ).astype(BF16)
    packed = -(-g_small.shape[1] * depth // (32 * width)) * 32
    g_small = jnp.pad(
        g_small.reshape(owners, -1), ((0, 0), (0, packed * width - g_small.shape[1] * depth))
    ).reshape(owners, packed, width)
    mine, other = patch_grad(core, resized, g_emb, g_small)
    kern = Sum(mine, other, reps, owners, over_reps[::-1] + others)
    mine, other = beside([kern], lambda d: qkv_grad(core, normed1, d, g_out), dproj)
    kern.land()
    if g_out.shape[0] == 1:
        both = jnp.concatenate([jnp.where(core == 0, mine, other), jnp.where(core == 0, other, mine)], axis=2)
        both = both.reshape(4, owners // 2, 2, depth, width).transpose(2, 1, 0, 3, 4)
        mine, other = jnp.where(core == 0, both[0], both[1]), jnp.where(core == 0, both[1], both[0])
    halves = (owners // 2, shard, width)
    qkvo = Sum(mine.reshape(halves), other.reshape(halves), reps, owners, over_reps[:1] + others + over_reps[1:])

    kern.kept, qkvo.kept = lax.optimization_barrier((kern.kept, qkvo.kept))
    qkvo.land()
    grad_pixels = None
    for channel in range(3):

        def work(pair):
            return unresize(
                lists, pair[0], groups, cats, ra, rb, resize_c, pixels.shape[1] // 3, channel, 0, 1, pair[1]
            )

        if channel == 2:
            g_emb = lax.optimization_barrier((g_emb, s_up))[0]
        grad_pixels = beside([qkvo, kern], work, (g_emb, grad_pixels))
        kern.land()
        qkvo.land()
    s_up, s_down = (lax.psum(p, "rep") for p in (s_up, s_down))
    while len(kern.back) > 1 or kern.steps:
        kern.land()
        qkvo.land()
    kern.kept, s_up, s_down = lax.optimization_barrier((kern.kept, s_up, s_down))
    s_up, s_down, grad_pixels, s_rest, s_kernel = lax.optimization_barrier(
        (s_up, s_down, grad_pixels, qkvo.total(), kern.total())
    )
    s_up, s_down, s_rest, s_kernel = (x.astype(F32) for x in (s_up, s_down, s_rest, s_kernel))
    s_small = s_kernel[shard:].reshape(-1)[: (9 + cells) * depth + shard].reshape(-1, depth)
    s_kernel = s_kernel[:shard]
    unstack = lambda p: p.reshape(-1, depth, width).transpose(1, 0, 2).reshape(depth, -1)
    return (
        output, grad_pixels, s_kernel, s_small[9 : 9 + cells], unstack(s_rest[: 3 * depth]),
        s_rest[3 * depth : 4 * depth], unstack(s_up), s_down,
        s_small[:7], s_small[9 + cells :].reshape(-1), s_small[7:9],
    )


def solution(mesh):
    tokens = P(("rep", "fsdp"), None)
    rows, columns = P("fsdp", None), P(None, "fsdp")
    in_specs = (
        tokens, tokens, P(), P(), P(), P(), P(), P(), tokens,
        rows, columns, rows, rows, rows, rows, columns, P("fsdp"), columns,
    )
    out_specs = (tokens, tokens, rows, columns, rows, rows, rows, rows, columns, P("fsdp"), columns)
    reps, owners = mesh.shape["rep"], mesh.shape["fsdp"]

    def here(*arrays):
        return local(reps, owners, *arrays)

    return jax.shard_map(here, mesh=mesh, in_specs=in_specs, out_specs=out_specs, check_vma=False)
```

```python
import jax
import jax.numpy as jnp
from jax import lax
from jax.experimental import pallas as pl
from jax.experimental.pallas import tpu as pltpu
from jax.sharding import PartitionSpec as P

HEADS = 12
GRID_A = 30
GRID_B = 10
GRID_C = 5
CHUNK = 16
TILE = 256
F32 = jnp.float32
BF16 = jnp.bfloat16
NEG = -1e30
SCALE = 0.125 * 1.4426950408889634
VMEM = 60 * 1024 * 1024


def nt(a, b):
    return lax.dot_general(a, b, (((1,), (1,)), ((), ())), preferred_element_type=F32)


def nn(a, b):
    return lax.dot_general(a, b, (((1,), (0,)), ((), ())), preferred_element_type=F32)


def tn(a, b):
    return lax.dot_general(a, b, (((0,), (0,)), ((), ())), preferred_element_type=F32)


def params(**more):
    return pltpu.CompilerParams(vmem_limit_bytes=VMEM, **more)


def cost(flops, moved, exps=0):
    return pl.CostEstimate(flops=int(flops), bytes_accessed=int(moved), transcendentals=int(exps))


def token_layout(classes, tokens_here):
    class_tokens = jnp.array(
        [GRID_A * GRID_A, GRID_B * GRID_B, GRID_C * GRID_C, 0], dtype=jnp.int32
    )
    class_ids = jnp.arange(4, dtype=jnp.int32)
    image_tokens = jnp.sum(
        jnp.where(classes[:, None] == class_ids[None, :], class_tokens[None, :], 0), axis=1
    )
    image_ends = jnp.cumsum(image_tokens)
    image_starts = image_ends - image_tokens
    positions = jnp.arange(tokens_here, dtype=jnp.int32)
    segment = jnp.sum((image_ends[None, :] <= positions[:, None]).astype(jnp.int32), axis=1)
    membership = segment[:, None] == jnp.arange(classes.shape[0], dtype=jnp.int32)[None, :]
    live_rows = jnp.any(membership, axis=1)
    category = jnp.sum(jnp.where(membership, classes[None, :], 0), axis=1) + jnp.where(
        live_rows, 0, 3
    )
    offset = positions - jnp.sum(jnp.where(membership, image_starts[None, :], 0), axis=1)
    return (segment, category, offset, live_rows)


def chunk_lists(category):
    chunks = category.reshape(-1, CHUNK)
    here = jnp.any(chunks[None, :, :] == jnp.arange(3, dtype=jnp.int32)[:, None, None], axis=2)
    place = jnp.cumsum(here.astype(jnp.int32), axis=1) - 1
    count = chunks.shape[0]
    ids = jnp.arange(count, dtype=jnp.int32)
    hit = here[:, :, None] & (place[:, :, None] == ids[None, None, :])
    listed = jnp.sum(jnp.where(hit, ids[None, :, None], 0), axis=1)
    return jnp.concatenate([place[:, -1:] + 1, listed], axis=1).astype(jnp.int32)


def resize_rows(lists, cat_ref, src_ref, out_ref, lhs, class_id, width, product, columns):
    number = lists[class_id, 0]

    @pl.loop(0, (number + TILE // CHUNK - 1) // (TILE // CHUNK))
    def _(t):
        base = t * (TILE // CHUNK)
        for u in range(TILE // CHUNK):
            row = pl.multiple_of(lists[class_id, 1 + jnp.minimum(base + u, number - 1)] * CHUNK, CHUNK)
            lhs[u * CHUNK : (u + 1) * CHUNK, 0:width] = src_ref[pl.ds(row, CHUNK), 0:width]
        total = product(lhs[:, 0:width])
        for u in range(TILE // CHUNK):

            @pl.when(base + u < number)
            def _():
                row = pl.multiple_of(lists[class_id, 1 + base + u] * CHUNK, CHUNK)
                mine = cat_ref[pl.ds(row, CHUNK), :] == class_id
                old = out_ref[pl.ds(row, CHUNK), 0:columns].astype(F32)
                new = total[u * CHUNK : (u + 1) * CHUNK, :]
                out_ref[pl.ds(row, CHUNK), 0:columns] = jnp.where(mine, new, old).astype(
                    out_ref.dtype
                )


def resize_kernel(lists, px_ref, cat_ref, ra_ref, rb_ref, rc_ref, out_ref, lhs):
    out_ref[...] = jnp.zeros_like(out_ref)
    for class_id, matrix in enumerate((ra_ref, rb_ref, rc_ref)):
        resize_rows(
            lists, cat_ref, px_ref, out_ref, lhs, class_id, matrix.shape[0],
            lambda rows, matrix=matrix: nn(rows, matrix[...]), matrix.shape[1],
        )


def resize(lists, pixels, category, ra, rb, rc):
    tokens, wide = pixels.shape
    area = wide // 3
    base = rc.shape[1]
    whole = lambda a: pl.BlockSpec(a.shape, lambda c, s: (0, 0))
    return pl.pallas_call(
        resize_kernel,
        grid_spec=pltpu.PrefetchScalarGridSpec(
            num_scalar_prefetch=1,
            grid=(3,),
            in_specs=[pl.BlockSpec((tokens, area), lambda c, s: (0, c)), whole(category), whole(ra), whole(rb), whole(rc)],
            out_specs=pl.BlockSpec((tokens, base), lambda c, s: (0, c)),
            scratch_shapes=[pltpu.VMEM((TILE, area), BF16)],
        ),
        out_shape=jax.ShapeDtypeStruct((tokens, 3 * base), BF16),
        compiler_params=params(),
        cost_estimate=cost(tokens * 3 * base * 1200 * 2, tokens * wide * 2 + tokens * base * 6),
        name="resize",
    )(lists, pixels, category, ra, rb, rc)


def unresize_kernel(lists, g_ref, w_ref, cat_ref, ra_ref, rb_ref, rc_ref, *rest):
    out_ref, grow, lhs = rest[-3:]
    out_ref[...] = jnp.zeros_like(out_ref)
    grow[...] = nt(g_ref[...], w_ref[0]).astype(BF16)
    for class_id, matrix in enumerate((ra_ref, rb_ref, rc_ref)):
        resize_rows(
            lists, cat_ref, grow, out_ref, lhs, class_id, grow.shape[1],
            lambda rows, matrix=matrix: nt(rows, matrix[...]), matrix.shape[0],
        )


def unresize(lists, g_emb, patch, category, ra, rb, rc, area, channel, part, parts, before):
    tokens, width = g_emb.shape
    base = rc.shape[1]
    rows = tokens // parts
    whole = lambda a: pl.BlockSpec(a.shape, lambda c, s: (0, 0))
    some = lambda a: pl.BlockSpec((rows, a.shape[1]), lambda c, s: (part, 0))
    kernels = patch.reshape(3, base, width)
    more = [] if before is None else [before]
    return pl.pallas_call(
        unresize_kernel,
        grid_spec=pltpu.PrefetchScalarGridSpec(
            num_scalar_prefetch=1,
            grid=(1,),
            in_specs=[
                some(g_emb), pl.BlockSpec((1, base, width), lambda c, s: (channel, 0, 0)),
                some(category), whole(ra), whole(rb), whole(rc),
            ] + [pl.BlockSpec(memory_space=pl.ANY)] * len(more),
            out_specs=pl.BlockSpec((rows, area), lambda c, s: (part, channel)),
            scratch_shapes=[pltpu.VMEM((rows, base), BF16), pltpu.VMEM((TILE, base), BF16)],
        ),
        out_shape=jax.ShapeDtypeStruct((tokens, 3 * area), BF16),
        input_output_aliases={7: 0} if more else {},
        compiler_params=params(),
        cost_estimate=cost(1e6, 1e5),
        name="unresize",
    )(lists, g_emb, kernels, category, ra, rb, rc, *more)


def norm_parts(values):
    center = values - jnp.mean(values, axis=-1, keepdims=True)
    rstd = lax.rsqrt(jnp.mean(center * center, axis=-1, keepdims=True) + 1e-06)
    return center * rstd, rstd


def norm_back(xhat, rstd, grad, gain):
    dxhat = grad * gain
    return rstd * (
        dxhat
        - jnp.mean(dxhat, axis=-1, keepdims=True)
        - xhat * jnp.mean(dxhat * xhat, axis=-1, keepdims=True)
    )


def square(ref):
    value = ref[...]
    return value.reshape(-1, value.shape[-1])


def row_tiles(tokens, body):
    body(pl.ds(0, tokens))


def embed_kernel(res_ref, kern_ref, pos_ref, table_ref, small_ref, embed_ref, norm_ref):
    step = pl.program_id(0)

    @pl.when(step == 0)
    def _():
        embed_ref[...] = (
            nn(res_ref[...], kern_ref[0]) + small_ref[0:1, :] + nn(pos_ref[...], table_ref[...])
        )

    @pl.when((step > 0) & (step < 3))
    def _():
        embed_ref[...] += nn(res_ref[...], kern_ref[0])

    @pl.when(step == 3)
    def _():
        value = embed_ref[...] + nn(res_ref[...], kern_ref[0])
        embed_ref[...] = value
        xhat, _ = norm_parts(value)
        norm_ref[...] = (xhat * small_ref[7:8, :] + small_ref[1:2, :]).astype(BF16)


def embed_call(resized, patch, pos_rows, table, small):
    tokens = resized.shape[0]
    width = small.shape[1]
    whole = lambda a: pl.BlockSpec(a.shape, lambda s: (0, 0))
    fixed = pl.BlockSpec((tokens, width), lambda s: (0, 0))
    return pl.pallas_call(
        embed_kernel,
        grid=(4,),
        in_specs=[
            pl.BlockSpec((tokens, width), lambda s: (0, s)),
            pl.BlockSpec((1, width, width), lambda s: (s, 0, 0)),
            whole(pos_rows), whole(table), whole(small),
        ],
        out_specs=[fixed, fixed],
        out_shape=[jax.ShapeDtypeStruct((tokens, width), F32), jax.ShapeDtypeStruct((tokens, width), BF16)],
        compiler_params=params(),
        cost_estimate=cost(4 * 2 * tokens * width * width, tokens * width * 14 + 4 * width * width * 2),
        name="embed",
    )(resized, patch.reshape(4, width, width), pos_rows, table, small)


def project_kernel(norm_ref, qkv_ref, small_ref, proj_ref):
    step = pl.program_id(0)
    none = jnp.zeros_like(small_ref[3:4, :])
    shift = jnp.where(step == 0, small_ref[2:3, :], jnp.where(step == 2, small_ref[3:4, :], none))
    proj_ref[...] = (nn(norm_ref[...], square(qkv_ref)) + shift).astype(BF16)


def project(normed1, colwise, small):
    tokens, width = normed1.shape
    bands, deep = colwise.shape[1], colwise.shape[3]
    whole = lambda a: pl.BlockSpec(a.shape, lambda s: (0, 0))
    return pl.pallas_call(
        project_kernel,
        grid=(3,),
        in_specs=[
            whole(normed1), pl.BlockSpec((1, bands, 1, deep, width), lambda s: (s, 0, 0, 0, 0)), whole(small),
        ],
        out_specs=pl.BlockSpec((tokens, width), lambda s: (0, s)),
        out_shape=jax.ShapeDtypeStruct((tokens, 3 * width), BF16),
        compiler_params=params(),
        cost_estimate=cost(3 * 2 * tokens * width * width, tokens * width * 8 + 3 * width * width * 2),
        name="project",
    )(normed1, colwise, small)


def half_roll(x):
    return jnp.concatenate([x[:, 64:128], x[:, 0:64]], axis=1)


def score_sides(q_ref, k_ref, tails, km_ref, qside, kside):
    lane = lax.broadcasted_iota(jnp.int32, (1, 128), 1)
    q = q_ref[...].astype(F32) * SCALE
    high = q.astype(BF16)
    low = half_roll((q - high.astype(F32)).astype(BF16))
    k = k_ref[...]
    turned = half_roll(k)
    for h in range(2):
        mine = (lane < 64) if h == 0 else (lane >= 64)
        qside[h, :, 0:128] = jnp.where(mine, high, low)
        qside[h, :, 128:256] = tails[h]
        kside[h, :, 0:128] = jnp.where(mine, k, turned)
        kside[h, :, 128:256] = km_ref[...]


def attend_kernel(q_ref, k_ref, v_ref, oh_ref, km_ref, o_ref, lse_ref, qside, kside, vside, kept, head_out, head_log):
    tokens = q_ref.shape[0]
    rows, cols = tokens // 2, tokens // 2
    lane = lax.broadcasted_iota(jnp.int32, (1, 128), 1)
    score_sides(q_ref, k_ref, [oh_ref[...]] * 2, km_ref, qside, kside)
    vside[:, 0:128] = v_ref[...]
    vside[:, 128:256] = jnp.ones((tokens, 128), BF16)
    units = [(t, h) for t in range(tokens // rows) for h in range(2)]
    chunks = [slice(c * cols, (c + 1) * cols) for c in range(tokens // cols)]

    def scores(unit, slot, chunk, top):
        t, h = unit
        value = nt(qside[h, t * rows : (t + 1) * rows, :], kside[h, chunk, :])
        kept[slot, :, chunk] = value
        for i in range(cols // 128):
            part = value[:, i * 128 : (i + 1) * 128]
            top = part if top is None else jnp.maximum(top, part)
        return top

    top = None
    for chunk in chunks:
        top = scores(units[0], 0, chunk, top)
    for u, (t, h) in enumerate(units):
        highest = jnp.max(top, axis=1, keepdims=True)
        top, total = None, None
        for chunk in chunks:
            if u + 1 < len(units):
                top = scores(units[u + 1], (u + 1) % 2, chunk, top)
            part = nn(jnp.exp2(kept[u % 2, :, chunk] - highest).astype(BF16), vside[chunk, :])
            total = part if total is None else total + part
        weight = total[:, 128:256]
        out, log = total[:, 0:128] / weight, highest + jnp.log2(weight)
        if h == 0:
            head_out[...] = out
            head_log[...] = log
        else:
            at = slice(t * rows, (t + 1) * rows)
            o_ref[at, :] = jnp.where(lane < 64, head_out[...], out).astype(BF16)
            lse_ref[at, :] = jnp.where(lane < 64, head_log[...], log)


def attend(projected, onehot, keymask):
    tokens = projected.shape[0]
    pairs = projected.shape[1] // 3 // 128
    part = lambda at: pl.BlockSpec((tokens, 128), lambda j: (0, at + j))
    whole = pl.BlockSpec((tokens, 128), lambda j: (0, 0))
    return pl.pallas_call(
        attend_kernel,
        grid=(pairs,),
        in_specs=[part(0), part(pairs), part(2 * pairs), whole, whole],
        out_specs=[part(0), part(0)],
        scratch_shapes=[
            pltpu.VMEM((2, tokens, 256), BF16), pltpu.VMEM((2, tokens, 256), BF16), pltpu.VMEM((tokens, 256), BF16),
            pltpu.VMEM((2, tokens // 2, tokens), F32),
            pltpu.VMEM((tokens // 2, 128), F32), pltpu.VMEM((tokens // 2, 128), F32),
        ],
        out_shape=[
            jax.ShapeDtypeStruct((tokens, pairs * 128), BF16),
            jax.ShapeDtypeStruct((tokens, pairs * 128), F32),
        ],
        compiler_params=params(),
        cost_estimate=cost(2 * 2 * 12 * tokens * tokens * 256, tokens * 2304 * 2 + tokens * 768 * 6, 12 * tokens * tokens),
        name="attend",
    )(projected, projected, projected, onehot, keymask)


def split3(x):
    high = x.astype(BF16)
    rest = x - high.astype(F32)
    middle = rest.astype(BF16)
    low = (rest - middle.astype(F32)).astype(BF16)
    return high, middle, low


def attend_back_kernel(
    q_ref, k_ref, v_ref, g_ref, o_ref, lse_ref, oh_ref, km_ref, out_ref,
    qside, kside, vside, gside, qhead, dkeys, dvals, kept, dprobs, dquery,
):
    tokens = q_ref.shape[0]
    rows, cols = tokens // 2, tokens // 2
    lane = lax.broadcasted_iota(jnp.int32, (1, 128), 1)

    def put(parts, at, other):
        for i, piece in enumerate(parts):
            other = jnp.where(lane == at + i, piece, other)
        return other

    lse = lse_ref[...]
    tails = [put(split3(lse[:, 64 * h : 64 * h + 1]), 64, oh_ref[...]) for h in range(2)]
    score_sides(q_ref, k_ref, tails, km_ref, qside, kside)
    vside[:, 0:128] = v_ref[...]
    vside[:, 128:256] = jnp.broadcast_to(jnp.where(lane < 3, -1.0, 0.0).astype(BF16), (tokens, 128))
    q = q_ref[...] * jnp.asarray(0.125, BF16)
    g = g_ref[...]
    go = g.astype(F32) * o_ref[...].astype(F32)
    for h in range(2):
        mine = (lane < 64) if h == 0 else (lane >= 64)
        delta = jnp.sum(jnp.where(mine, go, 0.0), axis=1, keepdims=True)
        gside[h, :, 0:128] = jnp.where(mine, g, jnp.zeros_like(g))
        gside[h, :, 128:256] = put(split3(delta), 0, jnp.zeros((tokens, 128), BF16))
        qhead[h] = jnp.where(mine, q, jnp.zeros_like(q))
    units = [(t, h) for t in range(tokens // rows) for h in range(2)]
    chunks = [slice(c * cols, (c + 1) * cols) for c in range(tokens // cols)]

    def first(unit, slot, chunk):
        t, h = unit
        at = slice(t * rows, (t + 1) * rows)
        kept[slot, chunk, :] = nt(kside[h, chunk, :], qside[h, at, :])
        dprobs[slot, chunk, :] = nt(vside[chunk, :], gside[h, at, :])

    for chunk in chunks:
        first(units[0], 0, chunk)
    for u, (t, h) in enumerate(units):
        at = slice(t * rows, (t + 1) * rows)
        dq = None
        for chunk in chunks:
            if u + 1 < len(units):
                first(units[u + 1], (u + 1) % 2, chunk)
            probs = jnp.exp2(kept[u % 2, chunk, :])
            dscores = (probs * dprobs[u % 2, chunk, :]).astype(BF16)
            dv, dk = nn(probs.astype(BF16), gside[h, at, 0:128]), nn(dscores, qhead[h, at, :])
            if u == 0:
                dvals[chunk, :] = dv
                dkeys[chunk, :] = dk
            else:
                dvals[chunk, :] += dv
                dkeys[chunk, :] += dk
            part = tn(dscores, k_ref[chunk, :])
            dq = part if dq is None else dq + part
        if h == 0:
            dquery[...] = dq
        else:
            out_ref[0, at, :] = (jnp.where(lane < 64, dquery[...], dq) * 0.125).astype(BF16)
    out_ref[1] = dkeys[...].astype(BF16)
    out_ref[2] = dvals[...].astype(BF16)


def attend_back(projected, g_mixed, mixed, lse, onehot, keymask):
    tokens = projected.shape[0]
    pairs = projected.shape[1] // 3 // 128
    part = lambda at: pl.BlockSpec((tokens, 128), lambda j: (0, at + j))
    whole = pl.BlockSpec((tokens, 128), lambda j: (0, 0))
    wide, narrow = pltpu.VMEM((2, tokens, 256), BF16), pltpu.VMEM((tokens, 128), F32)
    square_tile = pltpu.VMEM((2, tokens, tokens // 2), F32)
    return pl.pallas_call(
        attend_back_kernel,
        grid=(pairs,),
        in_specs=[part(0), part(pairs), part(2 * pairs), part(0), part(0), part(0), whole, whole],
        out_specs=pl.BlockSpec((3, tokens, 128), lambda j: (0, 0, j)),
        scratch_shapes=[
            wide, wide, pltpu.VMEM((tokens, 256), BF16), wide, pltpu.VMEM((2, tokens, 128), BF16),
            narrow, narrow, square_tile, square_tile, pltpu.VMEM((tokens // 2, 128), F32),
        ],
        out_shape=jax.ShapeDtypeStruct((3, tokens, pairs * 128), BF16),
        compiler_params=params(),
        cost_estimate=cost(5 * 2 * 12 * tokens * tokens * 256, tokens * 768 * 22, 12 * tokens * tokens),
        name="attend_back",
    )(projected, projected, projected, g_mixed, mixed, lse, onehot, keymask)


def mlp_kernel(
    embed_ref, mixed_ref, cot_ref, live_ref, small_ref, shift_ref, wo_ref, up_ref, down_ref,
    out_ref, ghid_ref, gmixed_ref, gdown_ref, gup_ref, gwo_ref, sums_ref, gshift_ref,
    hidden, xhats, norm2, gbranch, total, gnorm, act, gpre,
):
    step = pl.program_id(0)
    tokens = embed_ref.shape[0]

    @pl.when(step == 0)
    def _():
        def body(rows):
            value = embed_ref[rows, :] + nn(mixed_ref[rows, :], square(wo_ref)) + small_ref[4:5, :]
            hidden[rows, :] = value
            total[rows, :] = value + small_ref[6:7, :]
            xhat, _ = norm_parts(value)
            norm2[rows, :] = (xhat * small_ref[8:9, :] + small_ref[5:6, :]).astype(BF16)
            gbranch[rows, :] = (cot_ref[rows, :].astype(F32) * live_ref[rows, :]).astype(BF16)
            gnorm[rows, :] = jnp.zeros_like(value)

        row_tiles(tokens, body)

    up = square(up_ref)
    down = jnp.concatenate(
        [down_ref[r, f, 0] for f in range(down_ref.shape[1]) for r in range(down_ref.shape[0])]
    )

    def body(rows):
        x = nn(norm2[rows, :], up) + shift_ref[0]
        square_x = x * x
        t = jnp.tanh(0.7978845608028654 * (x + 0.044715 * (square_x * x)))
        half = 0.5 * (1.0 + t)
        acts = (x * half).astype(BF16)
        act[rows, :] = acts
        total[rows, :] += nn(acts, down)
        slope = half + 0.5 * x * (1.0 - t * t) * (
            0.7978845608028654 + (0.7978845608028654 * 3 * 0.044715) * square_x
        )
        gp = (nt(gbranch[rows, :], down) * slope).astype(BF16)
        gpre[rows, :] = gp
        gnorm[rows, :] += nt(gp, up)

    row_tiles(tokens, body)
    gdown_ref[0] = tn(act[...], gbranch[...]).astype(BF16)
    gup_ref[...] = tn(norm2[...], gpre[...]).astype(BF16).reshape(gup_ref.shape)
    gshift_ref[0] = jnp.sum(gpre[...].astype(F32), axis=0, keepdims=True)

    @pl.when(step == 3)
    def _():
        sums_ref[...] = jnp.zeros_like(sums_ref)
        wo = square(wo_ref)

        def body(rows):
            out_ref[rows, :] = (total[rows, :] * live_ref[rows, :]).astype(BF16)
            xhat, rstd = norm_parts(hidden[rows, :])
            grad = gnorm[rows, :]
            gout = gbranch[rows, :].astype(F32)
            ghid = gout + norm_back(xhat, rstd, grad, small_ref[8:9, :])
            ghid_ref[rows, :] = ghid
            gmix = ghid.astype(BF16)
            xhats[rows, :] = gmix
            gmixed_ref[rows, :] = nt(gmix, wo).astype(BF16)
            sums_ref[4:5, :] += jnp.sum(gmix.astype(F32), axis=0, keepdims=True)
            sums_ref[5:6, :] += jnp.sum(grad, axis=0, keepdims=True)
            sums_ref[6:7, :] += jnp.sum(gout, axis=0, keepdims=True)
            sums_ref[8:9, :] += jnp.sum(grad * xhat, axis=0, keepdims=True)

        row_tiles(tokens, body)
        gwo_ref[...] = tn(mixed_ref[...], xhats[...]).astype(BF16).reshape(gwo_ref.shape)


def mlp_call(embed, mixed, cotangent, live, small, shift, downs, colwise):
    tokens, width = embed.shape
    bands, deep = colwise.shape[1], colwise.shape[3]
    fixed = pl.BlockSpec((tokens, width), lambda s: (0, 0))
    whole = lambda a: pl.BlockSpec(a.shape, lambda s: (0, 0))
    band = lambda group, at: pl.BlockSpec((1, bands, 1, deep, width), lambda s: (at(s), 0, group, 0, 0))
    last = downs.shape[2] - 1
    down_block = (downs.shape[0], downs.shape[1] // 4, 1) + downs.shape[3:]
    scratch = lambda kind: pltpu.VMEM((tokens, width), kind)
    return pl.pallas_call(
        mlp_kernel,
        grid=(4,),
        in_specs=[
            fixed, fixed, fixed, whole(live), whole(small),
            pl.BlockSpec((1, 1, width), lambda s: (s, 0, 0)),
            band(0, lambda s: 3), band(1, lambda s: s),
            pl.BlockSpec(down_block, lambda s: (0, s, last, 0, 0)),
        ],
        out_specs=[
            fixed, fixed, fixed,
            pl.BlockSpec((1, width, width), lambda s: (s, 0, 0)),
            pl.BlockSpec((bands, 1, deep, width), lambda s: (0, s, 0, 0)),
            pl.BlockSpec((bands, deep, width), lambda s: (0, 0, 0)),
            pl.BlockSpec((16, width), lambda s: (0, 0)),
            pl.BlockSpec((1, 1, width), lambda s: (s, 0, 0)),
        ],
        out_shape=[
            jax.ShapeDtypeStruct((tokens, width), BF16),
            jax.ShapeDtypeStruct((tokens, width), F32),
            jax.ShapeDtypeStruct((tokens, width), BF16),
            jax.ShapeDtypeStruct((4, width, width), BF16),
            jax.ShapeDtypeStruct((bands, 4, deep, width), BF16),
            jax.ShapeDtypeStruct((bands, deep, width), BF16),
            jax.ShapeDtypeStruct((16, width), F32),
            jax.ShapeDtypeStruct((4, 1, width), F32),
        ],
        scratch_shapes=[
            scratch(F32), scratch(BF16), scratch(BF16), scratch(BF16),
            scratch(F32), scratch(F32), scratch(BF16), scratch(BF16),
        ],
        compiler_params=params(),
        cost_estimate=cost(27 * 2 * tokens * width * width, tokens * width * 20 + 18 * width * width * 2),
        name="mlp",
    )(embed, mixed, cotangent, live, small, shift, colwise, colwise, downs)


def store_split(core, value, mine_ref, other_ref):
    shape = mine_ref.shape
    pairs = value.reshape(-1, 2, shape[-2], shape[-1])
    first, second = pairs[:, 0].reshape(shape), pairs[:, 1].reshape(shape)

    @pl.when(core == 0)
    def _():
        mine_ref[...] = first
        other_ref[...] = second

    @pl.when(core != 0)
    def _():
        mine_ref[...] = second
        other_ref[...] = first


def qkv_grad_kernel(core_ref, norm_ref, dproj_ref, gwo_ref, mine_ref, other_ref):
    step = pl.program_id(0)

    @pl.when(step < 3)
    def _():
        value = tn(norm_ref[...], dproj_ref[0]).astype(BF16)
        store_split(core_ref[0], value, mine_ref, other_ref)

    @pl.when(step == 3)
    def _():
        store_split(core_ref[0], square(gwo_ref), mine_ref, other_ref)


def qkv_grad(core, normed1, dproj, g_out):
    tokens, width = normed1.shape
    bands, deep = g_out.shape[0], g_out.shape[1]
    half = (bands // 2, deep) if bands > 1 else (1, width // 2)
    pair = pl.BlockSpec((half[0], 1, half[1], width), lambda s, c: (0, s, 0, 0))
    shape = jax.ShapeDtypeStruct((half[0], 4, half[1], width), BF16)
    return pl.pallas_call(
        qkv_grad_kernel,
        grid_spec=pltpu.PrefetchScalarGridSpec(
            num_scalar_prefetch=1,
            grid=(4,),
            in_specs=[
                pl.BlockSpec((tokens, width), lambda s, c: (0, 0)),
                pl.BlockSpec((1, tokens, width), lambda s, c: (jnp.minimum(s, 2), 0, 0)),
                pl.BlockSpec(g_out.shape, lambda s, c: (0, 0, 0)),
            ],
            out_specs=[pair, pair],
        ),
        out_shape=[shape, shape],
        compiler_params=params(),
        cost_estimate=cost(1e6, 1e5),
        name="qkv_grad",
    )(core, normed1, dproj, g_out)


def embed_back_kernel(
    dproj_ref, qkv_ref, embed_ref, ghid_ref, pos_ref, small_ref, gemb_ref, gpos_ref, sums_ref, gnorm
):
    step = pl.program_id(0)
    tokens = embed_ref.shape[0]
    weight = square(qkv_ref)

    column = jnp.sum(dproj_ref[0].astype(F32), axis=0, keepdims=True)

    @pl.when(step == 0)
    def _():
        sums_ref[...] = jnp.zeros_like(sums_ref)
        sums_ref[2:3, :] = column

        def body(rows):
            gnorm[rows, :] = nt(dproj_ref[0, rows, :], weight)

        row_tiles(tokens, body)

    @pl.when(step == 1)
    def _():
        def body(rows):
            gnorm[rows, :] += nt(dproj_ref[0, rows, :], weight)

        row_tiles(tokens, body)

    @pl.when(step == 2)
    def _():
        sums_ref[3:4, :] = column

        def body(rows):
            grad = gnorm[rows, :] + nt(dproj_ref[0, rows, :], weight)
            xhat, rstd = norm_parts(embed_ref[rows, :])
            gemb = (ghid_ref[rows, :] + norm_back(xhat, rstd, grad, small_ref[7:8, :])).astype(BF16)
            gemb_ref[rows, :] = gemb
            sums_ref[0:1, :] += jnp.sum(gemb.astype(F32), axis=0, keepdims=True)
            sums_ref[1:2, :] += jnp.sum(grad, axis=0, keepdims=True)
            sums_ref[7:8, :] += jnp.sum(grad * xhat, axis=0, keepdims=True)

        row_tiles(tokens, body)
        gpos_ref[...] = tn(pos_ref[...], gemb_ref[...])


def embed_back(dproj, colwise, embed, g_hidden, pos_rows, small):
    tokens, width = embed.shape
    bands, deep = colwise.shape[1], colwise.shape[3]
    fixed = pl.BlockSpec((tokens, width), lambda s: (0, 0))
    whole = lambda a: pl.BlockSpec(a.shape, lambda s: (0, 0))
    return pl.pallas_call(
        embed_back_kernel,
        grid=(3,),
        in_specs=[
            pl.BlockSpec((1, tokens, width), lambda s: (s, 0, 0)),
            pl.BlockSpec((1, bands, 1, deep, width), lambda s: (s, 0, 0, 0, 0)),
            fixed, fixed, whole(pos_rows), whole(small),
        ],
        out_specs=[
            fixed, pl.BlockSpec((128, width), lambda s: (0, 0)), pl.BlockSpec((16, width), lambda s: (0, 0)),
        ],
        out_shape=[
            jax.ShapeDtypeStruct((tokens, width), BF16),
            jax.ShapeDtypeStruct((128, width), F32),
            jax.ShapeDtypeStruct((16, width), F32),
        ],
        scratch_shapes=[pltpu.VMEM((tokens, width), F32)],
        compiler_params=params(),
        cost_estimate=cost(1e6, 1e5),
        name="embed_back",
    )(dproj, colwise, embed, g_hidden, pos_rows, small)


def patch_grad_kernel(core_ref, res_ref, g_ref, small_ref, mine_ref, other_ref):
    shard = mine_ref.shape[1] - small_ref.shape[1]
    value = tn(res_ref[...], g_ref[...]).astype(BF16).reshape(-1, 2, shard, mine_ref.shape[2])
    tail = small_ref[...].reshape(-1, 2, small_ref.shape[1], small_ref.shape[2])

    def store(ref, which):
        ref[:, 0:shard, :] = value[:, which]
        ref[:, shard:, :] = tail[:, which]

    @pl.when(core_ref[0] == 0)
    def _():
        store(mine_ref, 0)
        store(other_ref, 1)

    @pl.when(core_ref[0] != 0)
    def _():
        store(mine_ref, 1)
        store(other_ref, 0)


def patch_grad(core, resized, g_emb, g_small):
    tokens, width = g_emb.shape
    owners, packed = g_small.shape[0], g_small.shape[1]
    shard = 4 * width // owners
    pair = pl.BlockSpec((owners // 8, shard + packed, width), lambda s, c: (s, 0, 0))
    shape = jax.ShapeDtypeStruct((owners // 2, shard + packed, width), BF16)
    return pl.pallas_call(
        patch_grad_kernel,
        grid_spec=pltpu.PrefetchScalarGridSpec(
            num_scalar_prefetch=1,
            grid=(4,),
            in_specs=[
                pl.BlockSpec((tokens, width), lambda s, c: (0, s)),
                pl.BlockSpec((tokens, width), lambda s, c: (0, 0)),
                pl.BlockSpec((owners // 4, packed, width), lambda s, c: (s, 0, 0)),
            ],
            out_specs=[pair, pair],
        ),
        out_shape=[shape, shape],
        compiler_params=params(),
        cost_estimate=cost(1e6, 1e5),
        name="patch_grad",
    )(core, resized, g_emb, g_small)


def finish_kernel(
    kern_ref, rest_ref, up_ref, down_ref,
    o_kern, o_qkv, o_out, o_up, o_down, o_biases, o_gains, o_pos, o_shift,
):
    shard, width = o_kern.shape
    depth = o_out.shape[0]
    kern = kern_ref[...].astype(F32)
    o_kern[...] = kern[0:shard]
    o_down[...] = down_ref[...].astype(F32)
    rest, up = rest_ref[...].astype(F32), up_ref[...].astype(F32)
    for j in range(4):
        rows, columns = slice(j * depth, (j + 1) * depth), slice(j * width, (j + 1) * width)
        o_up[:, columns] = up[rows]
        if j < 3:
            o_qkv[:, columns] = rest[rows]
        else:
            o_out[...] = rest[rows]
    small = jnp.concatenate([kern[shard:, 0:128], kern[shard:, 128:256]])[:, 0:depth]
    at = 0
    for ref in (o_biases, o_gains, o_pos, o_shift):
        ref[...] = small[at : at + ref.shape[0]]
        at += ref.shape[0]


def finish(kern, rest, up, down, cells):
    shard, width = down.shape
    depth = shard // 4
    shapes = [
        (shard, width), (depth, 3 * width), (depth, width), (depth, 4 * width), (shard, width),
        (7, depth), (2, depth), (cells, depth), (4, depth),
    ]
    return pl.pallas_call(
        finish_kernel,
        out_shape=[jax.ShapeDtypeStruct(shape, F32) for shape in shapes],
        compiler_params=params(),
        name="finish",
    )(kern, rest, up, down)


def bit_of(axis, bit):
    return (lax.axis_index(axis) >> bit) & 1


class Sum:
    def __init__(self, mine, other, reps, owners, steps):
        self.sizes = dict(rep=reps, fsdp=owners)
        self.lead = [("fsdp", b) for b in range(1, owners.bit_length() - 1)][::-1]
        self.steps = [("fsdp", 0)] + steps
        self.back = [s for s in steps if s[0] == "rep"][::-1]
        shape = (2,) * len(self.lead) + mine.shape[1:]
        self.launch(mine.reshape(shape), other.reshape(shape))

    def launch(self, kept, sent):
        axis, bit = (self.steps or self.back)[0]
        pairs = [(i, i ^ (1 << bit)) for i in range(self.sizes[axis])]
        kept, sent = lax.optimization_barrier((kept, sent))
        self.kept, self.flying = kept, lax.ppermute(sent, axis, pairs)

    def land(self):
        if not self.steps and not self.back:
            return
        if self.steps:
            self.steps.pop(0)
            value = (self.kept.astype(F32) + self.flying.astype(F32)).astype(BF16)
        else:
            axis, bit = self.back.pop(0)
            low = bit_of(axis, bit) == 0
            a, b = self.kept, self.flying
            value = jnp.concatenate([jnp.where(low, a, b), jnp.where(low, b, a)])
        if self.steps:
            axis, bit = self.steps[0]
            if axis == "fsdp":
                at = self.lead.index((axis, bit))
                self.lead.remove((axis, bit))
            else:
                at = len(self.lead)
                value = value.reshape(value.shape[:at] + (2, value.shape[at] // 2) + value.shape[at + 1 :])
            mine = bit_of(axis, bit)
            pick = lambda i: lax.dynamic_index_in_dim(value, i, at, keepdims=False)
            self.launch(pick(mine), pick(1 - mine))
        elif self.back:
            self.launch(value, value)
        else:
            self.kept = value

    def total(self):
        while self.steps or self.back:
            self.land()
        return self.kept


class Gather:
    def __init__(self, shard, reps, owners, flip=False):
        rep, own = reps.bit_length() - 1, owners.bit_length() - 1
        self.sizes = dict(rep=reps, fsdp=owners)
        self.order = [("fsdp", b) for b in range(own)][::-1] + [("rep", b) for b in range(rep)][::-1]
        over_reps = self.order[own:][::-1] if flip else self.order[own:]
        self.steps = self.order[: own - 1] + over_reps + [("fsdp", 0)]
        self.held = []
        self.shape = (owners * shard.shape[0], shard.shape[1])
        share = shard.shape[0] // reps
        at = lax.axis_index("rep") * share if reps > 1 else 0
        self.launch(lax.dynamic_slice(shard, (at, 0), (share, shard.shape[1])))

    def launch(self, value):
        self.kept = value
        if self.steps:
            axis, bit = self.steps[0]
            self.flying = lax.ppermute(value, axis, [(i, i ^ (1 << bit)) for i in range(self.sizes[axis])])

    def land(self):
        if not self.steps:
            return
        axis, bit = self.steps.pop(0)
        at = sum(self.order.index(h) < self.order.index((axis, bit)) for h in self.held)
        self.held.append((axis, bit))
        low = bit_of(axis, bit) == 0
        a, b = self.kept, self.flying
        self.launch(jnp.stack([jnp.where(low, a, b), jnp.where(low, b, a)], axis=at))

    def total(self):
        while self.steps:
            self.land()
        return self.kept.reshape(self.shape)


def beside(sums, work, value):
    value = lax.optimization_barrier((value, *[one.kept for one in sums]))[0]
    value, *kept = lax.optimization_barrier((work(value), *[one.kept for one in sums]))
    for one, k in zip(sums, kept):
        one.kept = k
    return value


def local(reps, owners, *arrays):
    (
        pixels, image_class, resize_a, resize_b, resize_c, posmap_a, posmap_b, posmap_c, cotangent,
        patch_kernel, pos_table, qkv_weight, out_weight, up_weight, down_weight, biases, up_bias, gains,
    ) = arrays
    tokens = pixels.shape[0]
    width = out_weight.shape[1]
    depth = out_weight.shape[0]
    shard = patch_kernel.shape[0]
    cells = pos_table.shape[0]
    slots = image_class.shape[1]

    def stacked(shards):
        return jnp.concatenate([w.reshape(depth, -1, width).transpose(1, 0, 2) for w in shards]).reshape(shard, width)

    small_here = jnp.concatenate([biases, gains, pos_table, up_bias.reshape(-1, depth)])
    here_rows = small_here.shape[0]
    small_here = jnp.pad(small_here, ((0, -here_rows % 16), (0, 0)))
    bundle = jnp.stack([stacked([qkv_weight, out_weight]), stacked([up_weight]), down_weight])
    share = shard // reps
    here = lax.dynamic_slice(bundle, (0, lax.axis_index("rep") * share, 0), (3, share, width))
    groups = lax.all_gather(here, ("rep", "fsdp"), axis=0, tiled=False).reshape(reps, owners, 3, share, width)
    kernel = Gather(patch_kernel, reps, owners)
    little = Gather(small_here, 1, owners)
    while len(kernel.steps) > 2:
        kernel.land()
        little.land()
    small_all = little.total().reshape(owners, -1, depth)[:, :here_rows]
    if reps == 4 and depth % 16 == 0 and owners % 4 == 0:
        colwise = downs = groups
    else:
        groups = groups.transpose(2, 1, 0, 3, 4).reshape(3, owners, shard, width)
        colwise = groups.reshape(3, owners, 4, depth, width).transpose(2, 0, 1, 3, 4).reshape(4, 1, 3, width, width)
        downs = groups[2].reshape(1, 4, 1, width, width)
    rows_of = small_all[:, : 9 + cells].transpose(1, 0, 2).reshape(9 + cells, width)
    small = jnp.pad(rows_of[:9].astype(F32), ((0, 7), (0, 0)))
    table = jnp.pad(rows_of[9:], ((0, 128 - cells), (0, 0)))
    shift = small_all[:, 9 + cells :].reshape(4, 1, width).astype(F32)

    segment, category, offset, live_rows = token_layout(image_class[0], tokens)
    live = live_rows[:, None].astype(F32)
    lists = chunk_lists(category)
    lane = jnp.arange(128, dtype=jnp.int32)[None, :]
    same = segment[:, None] == lane
    onehot = same.astype(BF16)
    keymask = jnp.where(
        lane <= slots, jnp.where(same, 0.0, NEG), jnp.where((lane >= 64) & (lane < 67), -1.0, 0.0)
    ).astype(BF16)
    maps = jnp.concatenate([posmap_a, posmap_b, posmap_c, jnp.zeros((1, cells), BF16)])
    maps = jnp.pad(maps, ((0, 0), (0, 128 - cells)))
    first = jnp.array([0, GRID_A * GRID_A, GRID_A * GRID_A + GRID_B * GRID_B], jnp.int32)
    at = jnp.where(category < 3, first[jnp.minimum(category, 2)] + offset, maps.shape[0] - 1)
    pos_rows = jnp.take(maps, at, axis=0)
    cats = category[:, None]
    ra = jnp.pad(resize_a, ((0, -resize_a.shape[0] % 128), (0, 0)))
    rb = jnp.pad(resize_b, ((0, -resize_b.shape[0] % 128), (0, 0)))

    resized = beside([kernel], lambda p: resize(lists, p, cats, ra, rb, resize_c), pixels)
    patch = kernel.total()
    embed, normed1 = embed_call(resized, patch, pos_rows, table, small)
    projected = project(normed1, colwise, small)
    mixed, lse = attend(projected, onehot, keymask)
    output, g_hidden, g_mixed, g_down, g_up, g_out, sums_mlp, g_shift = mlp_call(
        embed, mixed, cotangent, live, small, shift, downs, colwise
    )
    def bands_of(blocks, number):
        if blocks.shape[0] != owners:
            blocks = blocks.reshape(number, owners, depth, width).transpose(1, 0, 2, 3)
        return blocks.reshape(owners, number * depth, width)

    scatter = lambda x: lax.psum_scatter(x, "fsdp", scatter_dimension=0, tiled=False)
    s_down = scatter(g_down.reshape(owners, shard, width))
    s_up = scatter(bands_of(g_up, 4))
    dproj = attend_back(projected, g_mixed, mixed, lse, onehot, keymask)
    core = bit_of("fsdp", 0).reshape(1)
    own, rep = owners.bit_length() - 1, reps.bit_length() - 1
    others = [("fsdp", b) for b in range(1, own)]
    over_reps = [("rep", b) for b in range(rep)]
    g_emb, g_pos, sums_embed = embed_back(dproj, colwise, embed, g_hidden, pos_rows, small)
    lanes = ((0, 0), (0, 0), (0, 128 - depth))
    g_small = jnp.concatenate([(sums_mlp + sums_embed)[:9], g_pos[:cells]]).reshape(9 + cells, owners, depth)
    g_small = jnp.concatenate(
        [jnp.pad(g_small, lanes).transpose(1, 0, 2), jnp.pad(g_shift.reshape(owners, 4, depth), lanes)], axis=1
    ).astype(BF16)
    g_small = jnp.pad(g_small, ((0, 0), (0, 64 - g_small.shape[1]), (0, 0)))
    g_small = jnp.concatenate([g_small[:, :32], g_small[:, 32:], jnp.zeros((owners, 32, width - 256), BF16)], axis=2)
    mine, other = patch_grad(core, resized, g_emb, g_small)
    kern = Sum(mine, other, reps, owners, over_reps[::-1] + others)
    mine, other = beside([kern], lambda d: qkv_grad(core, normed1, d, g_out), dproj)
    kern.land()
    if g_out.shape[0] == 1:
        both = jnp.concatenate([jnp.where(core == 0, mine, other), jnp.where(core == 0, other, mine)], axis=2)
        both = both.reshape(4, owners // 2, 2, depth, width).transpose(2, 1, 0, 3, 4)
        mine, other = jnp.where(core == 0, both[0], both[1]), jnp.where(core == 0, both[1], both[0])
    halves = (owners // 2, shard, width)
    qkvo = Sum(mine.reshape(halves), other.reshape(halves), reps, owners, over_reps[:1] + others + over_reps[1:])

    kern.kept, qkvo.kept = lax.optimization_barrier((kern.kept, qkvo.kept))
    qkvo.land()
    g_emb = lax.optimization_barrier((g_emb, s_down))[0]
    grad_pixels = None
    for channel in range(3):

        def work(pair):
            return unresize(
                lists, pair[0], patch, cats, ra, rb, resize_c, pixels.shape[1] // 3, channel, 0, 1, pair[1]
            )

        if channel == 1:
            g_emb = lax.optimization_barrier((g_emb, s_up))[0]
        grad_pixels = beside([qkvo, kern], work, (g_emb, grad_pixels))
        kern.land()
        qkvo.land()
    s_up, s_down = (lax.psum(p, "rep") for p in (s_up, s_down))
    while len(kern.back) > 1 or kern.steps:
        kern.land()
        qkvo.land()
    kern.kept, s_up, s_down = lax.optimization_barrier((kern.kept, s_up, s_down))
    totals = finish(kern.total(), qkvo.total(), s_up, s_down, cells)
    t_kernel, t_qkv, t_out, t_up, t_down, t_biases, t_gains, t_pos, t_shift = totals
    return (
        output, grad_pixels, t_kernel, t_pos, t_qkv, t_out, t_up, t_down, t_biases, t_shift.reshape(-1), t_gains
    )


def solution(mesh):
    tokens = P(("rep", "fsdp"), None)
    rows, columns = P("fsdp", None), P(None, "fsdp")
    in_specs = (
        tokens, tokens, P(), P(), P(), P(), P(), P(), tokens,
        rows, columns, rows, rows, rows, rows, columns, P("fsdp"), columns,
    )
    out_specs = (tokens, tokens, rows, columns, rows, rows, rows, rows, columns, P("fsdp"), columns)
    reps, owners = mesh.shape["rep"], mesh.shape["fsdp"]

    def here(*arrays):
        return local(reps, owners, *arrays)

    return jax.shard_map(here, mesh=mesh, in_specs=in_specs, out_specs=out_specs, check_vma=False)
```

```python
import jax
import jax.numpy as jnp
from jax import lax
from jax.experimental import pallas as pl
from jax.experimental.pallas import tpu as pltpu
from jax.sharding import PartitionSpec as P

HEADS = 12
GRID_A = 30
GRID_B = 10
GRID_C = 5
CHUNK = 16
TILE = 256
F32 = jnp.float32
BF16 = jnp.bfloat16
NEG = -1e30
SCALE = 0.125 * 1.4426950408889634
VMEM = 60 * 1024 * 1024


def nt(a, b):
    return lax.dot_general(a, b, (((1,), (1,)), ((), ())), preferred_element_type=F32)


def nn(a, b):
    return lax.dot_general(a, b, (((1,), (0,)), ((), ())), preferred_element_type=F32)


def tn(a, b):
    return lax.dot_general(a, b, (((0,), (0,)), ((), ())), preferred_element_type=F32)


def params(**more):
    return pltpu.CompilerParams(vmem_limit_bytes=VMEM, **more)


def cost(flops, moved, exps=0):
    return pl.CostEstimate(flops=int(flops), bytes_accessed=int(moved), transcendentals=int(exps))


def token_layout(classes, tokens_here):
    class_tokens = jnp.array(
        [GRID_A * GRID_A, GRID_B * GRID_B, GRID_C * GRID_C, 0], dtype=jnp.int32
    )
    class_ids = jnp.arange(4, dtype=jnp.int32)
    image_tokens = jnp.sum(
        jnp.where(classes[:, None] == class_ids[None, :], class_tokens[None, :], 0), axis=1
    )
    image_ends = jnp.cumsum(image_tokens)
    image_starts = image_ends - image_tokens
    positions = jnp.arange(tokens_here, dtype=jnp.int32)
    segment = jnp.sum((image_ends[None, :] <= positions[:, None]).astype(jnp.int32), axis=1)
    membership = segment[:, None] == jnp.arange(classes.shape[0], dtype=jnp.int32)[None, :]
    live_rows = jnp.any(membership, axis=1)
    category = jnp.sum(jnp.where(membership, classes[None, :], 0), axis=1) + jnp.where(
        live_rows, 0, 3
    )
    offset = positions - jnp.sum(jnp.where(membership, image_starts[None, :], 0), axis=1)
    return (segment, category, offset, live_rows)


def chunk_lists(category):
    chunks = category.reshape(-1, CHUNK)
    here = jnp.any(chunks[None, :, :] == jnp.arange(3, dtype=jnp.int32)[:, None, None], axis=2)
    place = jnp.cumsum(here.astype(jnp.int32), axis=1) - 1
    count = chunks.shape[0]
    ids = jnp.arange(count, dtype=jnp.int32)
    hit = here[:, :, None] & (place[:, :, None] == ids[None, None, :])
    listed = jnp.sum(jnp.where(hit, ids[None, :, None], 0), axis=1)
    return jnp.concatenate([place[:, -1:] + 1, listed], axis=1).astype(jnp.int32)


def resize_rows(lists, cat_ref, src_ref, out_ref, lhs, class_id, width, product, columns, fresh):
    number = lists[class_id, 0]

    @pl.loop(0, (number + TILE // CHUNK - 1) // (TILE // CHUNK))
    def _(t):
        base = t * (TILE // CHUNK)
        for u in range(TILE // CHUNK):
            row = pl.multiple_of(lists[class_id, 1 + jnp.minimum(base + u, number - 1)] * CHUNK, CHUNK)
            lhs[u * CHUNK : (u + 1) * CHUNK, 0:width] = src_ref[pl.ds(row, CHUNK), 0:width]
        total = product(lhs[:, 0:width])
        for u in range(TILE // CHUNK):

            @pl.when(base + u < number)
            def _():
                row = pl.multiple_of(lists[class_id, 1 + base + u] * CHUNK, CHUNK)
                mine = cat_ref[pl.ds(row, CHUNK), :] == class_id
                if fresh:
                    old = jnp.zeros((CHUNK, columns), F32)
                else:
                    old = out_ref[pl.ds(row, CHUNK), 0:columns].astype(F32)
                new = total[u * CHUNK : (u + 1) * CHUNK, :]
                out_ref[pl.ds(row, CHUNK), 0:columns] = jnp.where(mine, new, old).astype(
                    out_ref.dtype
                )


def resize_kernel(lists, px_ref, cat_ref, ra_ref, rb_ref, rc_ref, out_ref, lhs):
    out_ref[...] = jnp.zeros_like(out_ref)
    for class_id, matrix in ((2, rc_ref), (1, rb_ref), (0, ra_ref)):
        resize_rows(
            lists, cat_ref, px_ref, out_ref, lhs, class_id, matrix.shape[0],
            lambda rows, matrix=matrix: nn(rows, matrix[...]), matrix.shape[1], class_id == 2,
        )


def resize(lists, pixels, category, ra, rb, rc):
    tokens, wide = pixels.shape
    area = wide // 3
    base = rc.shape[1]
    whole = lambda a: pl.BlockSpec(a.shape, lambda c, s: (0, 0))
    return pl.pallas_call(
        resize_kernel,
        grid_spec=pltpu.PrefetchScalarGridSpec(
            num_scalar_prefetch=1,
            grid=(3,),
            in_specs=[pl.BlockSpec((tokens, area), lambda c, s: (0, c)), whole(category), whole(ra), whole(rb), whole(rc)],
            out_specs=pl.BlockSpec((tokens, base), lambda c, s: (0, c)),
            scratch_shapes=[pltpu.VMEM((TILE, area), BF16)],
        ),
        out_shape=jax.ShapeDtypeStruct((tokens, 3 * base), BF16),
        compiler_params=params(),
        cost_estimate=cost(tokens * 3 * base * 1200 * 2, tokens * wide * 2 + tokens * base * 6),
        name="resize",
    )(lists, pixels, category, ra, rb, rc)


def unresize_kernel(lists, g_ref, w_ref, cat_ref, ra_ref, rb_ref, rc_ref, *rest):
    out_ref, grow, lhs = rest[-3:]
    out_ref[...] = jnp.zeros_like(out_ref)
    grow[...] = nt(g_ref[...], w_ref[0]).astype(BF16)
    for class_id, matrix in ((2, rc_ref), (1, rb_ref), (0, ra_ref)):
        resize_rows(
            lists, cat_ref, grow, out_ref, lhs, class_id, grow.shape[1],
            lambda rows, matrix=matrix: nt(rows, matrix[...]), matrix.shape[0], class_id == 2,
        )


def unresize(lists, g_emb, patch, category, ra, rb, rc, area, channel, part, parts, before):
    tokens, width = g_emb.shape
    base = rc.shape[1]
    rows = tokens // parts
    whole = lambda a: pl.BlockSpec(a.shape, lambda c, s: (0, 0))
    some = lambda a: pl.BlockSpec((rows, a.shape[1]), lambda c, s: (part, 0))
    kernels = patch.reshape(3, base, width)
    more = [] if before is None else [before]
    return pl.pallas_call(
        unresize_kernel,
        grid_spec=pltpu.PrefetchScalarGridSpec(
            num_scalar_prefetch=1,
            grid=(1,),
            in_specs=[
                some(g_emb), pl.BlockSpec((1, base, width), lambda c, s: (channel, 0, 0)),
                some(category), whole(ra), whole(rb), whole(rc),
            ] + [pl.BlockSpec(memory_space=pl.ANY)] * len(more),
            out_specs=pl.BlockSpec((rows, area), lambda c, s: (part, channel)),
            scratch_shapes=[pltpu.VMEM((rows, base), BF16), pltpu.VMEM((TILE, base), BF16)],
        ),
        out_shape=jax.ShapeDtypeStruct((tokens, 3 * area), BF16),
        input_output_aliases={7: 0} if more else {},
        compiler_params=params(),
        cost_estimate=cost(1e6, 1e5),
        name="unresize",
    )(lists, g_emb, kernels, category, ra, rb, rc, *more)


def norm_parts(values):
    center = values - jnp.mean(values, axis=-1, keepdims=True)
    rstd = lax.rsqrt(jnp.mean(center * center, axis=-1, keepdims=True) + 1e-06)
    return center * rstd, rstd


def norm_back(xhat, rstd, grad, gain):
    dxhat = grad * gain
    return rstd * (
        dxhat
        - jnp.mean(dxhat, axis=-1, keepdims=True)
        - xhat * jnp.mean(dxhat * xhat, axis=-1, keepdims=True)
    )


def square(ref):
    value = ref[...]
    return value.reshape(-1, value.shape[-1])


def row_tiles(tokens, body):
    body(pl.ds(0, tokens))


def embed_kernel(res_ref, kern_ref, pos_ref, table_ref, small_ref, embed_ref, norm_ref):
    step = pl.program_id(0)

    @pl.when(step == 0)
    def _():
        embed_ref[...] = (
            nn(res_ref[...], kern_ref[0]) + small_ref[0:1, :] + nn(pos_ref[...], table_ref[...])
        )

    @pl.when((step > 0) & (step < 3))
    def _():
        embed_ref[...] += nn(res_ref[...], kern_ref[0])

    @pl.when(step == 3)
    def _():
        value = embed_ref[...] + nn(res_ref[...], kern_ref[0])
        embed_ref[...] = value
        xhat, _ = norm_parts(value)
        norm_ref[...] = (xhat * small_ref[7:8, :] + small_ref[1:2, :]).astype(BF16)


def embed_call(resized, patch, pos_rows, table, small):
    tokens = resized.shape[0]
    width = small.shape[1]
    whole = lambda a: pl.BlockSpec(a.shape, lambda s: (0, 0))
    fixed = pl.BlockSpec((tokens, width), lambda s: (0, 0))
    return pl.pallas_call(
        embed_kernel,
        grid=(4,),
        in_specs=[
            pl.BlockSpec((tokens, width), lambda s: (0, s)),
            pl.BlockSpec((1, width, width), lambda s: (s, 0, 0)),
            whole(pos_rows), whole(table), whole(small),
        ],
        out_specs=[fixed, fixed],
        out_shape=[jax.ShapeDtypeStruct((tokens, width), F32), jax.ShapeDtypeStruct((tokens, width), BF16)],
        compiler_params=params(),
        cost_estimate=cost(4 * 2 * tokens * width * width, tokens * width * 14 + 4 * width * width * 2),
        name="embed",
    )(resized, patch.reshape(4, width, width), pos_rows, table, small)


def project_kernel(norm_ref, qkv_ref, small_ref, proj_ref):
    step = pl.program_id(0)
    none = jnp.zeros_like(small_ref[3:4, :])
    shift = jnp.where(step == 0, small_ref[2:3, :], jnp.where(step == 2, small_ref[3:4, :], none))
    proj_ref[...] = (nn(norm_ref[...], square(qkv_ref)) + shift).astype(BF16)


def project(normed1, colwise, small):
    tokens, width = normed1.shape
    bands, deep = colwise.shape[1], colwise.shape[3]
    whole = lambda a: pl.BlockSpec(a.shape, lambda s: (0, 0))
    return pl.pallas_call(
        project_kernel,
        grid=(3,),
        in_specs=[
            whole(normed1), pl.BlockSpec((1, bands, 1, deep, width), lambda s: (s, 0, 0, 0, 0)), whole(small),
        ],
        out_specs=pl.BlockSpec((tokens, width), lambda s: (0, s)),
        out_shape=jax.ShapeDtypeStruct((tokens, 3 * width), BF16),
        compiler_params=params(),
        cost_estimate=cost(3 * 2 * tokens * width * width, tokens * width * 8 + 3 * width * width * 2),
        name="project",
    )(normed1, colwise, small)


def half_roll(x):
    return jnp.concatenate([x[:, 64:128], x[:, 0:64]], axis=1)


def score_sides(q_ref, k_ref, tails, km_ref, qside, kside):
    lane = lax.broadcasted_iota(jnp.int32, (1, 128), 1)
    q = q_ref[...].astype(F32) * SCALE
    high = q.astype(BF16)
    low = half_roll((q - high.astype(F32)).astype(BF16))
    k = k_ref[...]
    turned = half_roll(k)
    for h in range(2):
        mine = (lane < 64) if h == 0 else (lane >= 64)
        qside[h, :, 0:128] = jnp.where(mine, high, low)
        qside[h, :, 128:256] = tails[h]
        kside[h, :, 0:128] = jnp.where(mine, k, turned)
        kside[h, :, 128:256] = km_ref[...]


def attend_kernel(q_ref, k_ref, v_ref, oh_ref, km_ref, o_ref, lse_ref, qside, kside, vside, kept, head_out, head_log):
    tokens = q_ref.shape[0]
    rows, cols = tokens // 2, tokens // 2
    lane = lax.broadcasted_iota(jnp.int32, (1, 128), 1)
    score_sides(q_ref, k_ref, [oh_ref[...]] * 2, km_ref, qside, kside)
    vside[:, 0:128] = v_ref[...]
    vside[:, 128:256] = jnp.ones((tokens, 128), BF16)
    units = [(t, h) for t in range(tokens // rows) for h in range(2)]
    chunks = [slice(c * cols, (c + 1) * cols) for c in range(tokens // cols)]

    def scores(unit, slot, chunk, top):
        t, h = unit
        value = nt(qside[h, t * rows : (t + 1) * rows, :], kside[h, chunk, :])
        kept[slot, :, chunk] = value
        for i in range(cols // 128):
            part = value[:, i * 128 : (i + 1) * 128]
            top = part if top is None else jnp.maximum(top, part)
        return top

    top = None
    for chunk in chunks:
        top = scores(units[0], 0, chunk, top)
    for u, (t, h) in enumerate(units):
        highest = jnp.max(top, axis=1, keepdims=True)
        top, total = None, None
        for chunk in chunks:
            if u + 1 < len(units):
                top = scores(units[u + 1], (u + 1) % 2, chunk, top)
            part = nn(jnp.exp2(kept[u % 2, :, chunk] - highest).astype(BF16), vside[chunk, :])
            total = part if total is None else total + part
        weight = total[:, 128:256]
        out, log = total[:, 0:128] / weight, highest + jnp.log2(weight)
        if h == 0:
            head_out[...] = out
            head_log[...] = log
        else:
            at = slice(t * rows, (t + 1) * rows)
            o_ref[at, :] = jnp.where(lane < 64, head_out[...], out).astype(BF16)
            lse_ref[at, :] = jnp.where(lane < 64, head_log[...], log)


def attend(projected, onehot, keymask):
    tokens = projected.shape[0]
    pairs = projected.shape[1] // 3 // 128
    part = lambda at: pl.BlockSpec((tokens, 128), lambda j: (0, at + j))
    whole = pl.BlockSpec((tokens, 128), lambda j: (0, 0))
    return pl.pallas_call(
        attend_kernel,
        grid=(pairs,),
        in_specs=[part(0), part(pairs), part(2 * pairs), whole, whole],
        out_specs=[part(0), part(0)],
        scratch_shapes=[
            pltpu.VMEM((2, tokens, 256), BF16), pltpu.VMEM((2, tokens, 256), BF16), pltpu.VMEM((tokens, 256), BF16),
            pltpu.VMEM((2, tokens // 2, tokens), F32),
            pltpu.VMEM((tokens // 2, 128), F32), pltpu.VMEM((tokens // 2, 128), F32),
        ],
        out_shape=[
            jax.ShapeDtypeStruct((tokens, pairs * 128), BF16),
            jax.ShapeDtypeStruct((tokens, pairs * 128), F32),
        ],
        compiler_params=params(),
        cost_estimate=cost(2 * 2 * 12 * tokens * tokens * 256, tokens * 2304 * 2 + tokens * 768 * 6, 12 * tokens * tokens),
        name="attend",
    )(projected, projected, projected, onehot, keymask)


def split3(x):
    high = x.astype(BF16)
    rest = x - high.astype(F32)
    middle = rest.astype(BF16)
    low = (rest - middle.astype(F32)).astype(BF16)
    return high, middle, low


def attend_back_kernel(
    q_ref, k_ref, v_ref, g_ref, o_ref, lse_ref, oh_ref, km_ref, out_ref,
    qside, kside, vside, gside, qhead, dkeys, dvals, kept, dprobs, dquery,
):
    tokens = q_ref.shape[0]
    rows, cols = tokens // 2, tokens // 2
    lane = lax.broadcasted_iota(jnp.int32, (1, 128), 1)

    def put(parts, at, other):
        for i, piece in enumerate(parts):
            other = jnp.where(lane == at + i, piece, other)
        return other

    lse = lse_ref[...]
    tails = [put(split3(lse[:, 64 * h : 64 * h + 1]), 64, oh_ref[...]) for h in range(2)]
    score_sides(q_ref, k_ref, tails, km_ref, qside, kside)
    vside[:, 0:128] = v_ref[...]
    vside[:, 128:256] = jnp.broadcast_to(jnp.where(lane < 3, -1.0, 0.0).astype(BF16), (tokens, 128))
    q = q_ref[...] * jnp.asarray(0.125, BF16)
    g = g_ref[...]
    go = g.astype(F32) * o_ref[...].astype(F32)
    for h in range(2):
        mine = (lane < 64) if h == 0 else (lane >= 64)
        delta = jnp.sum(jnp.where(mine, go, 0.0), axis=1, keepdims=True)
        gside[h, :, 0:128] = jnp.where(mine, g, jnp.zeros_like(g))
        gside[h, :, 128:256] = put(split3(delta), 0, jnp.zeros((tokens, 128), BF16))
        qhead[h] = jnp.where(mine, q, jnp.zeros_like(q))
    units = [(t, h) for t in range(tokens // rows) for h in range(2)]
    chunks = [slice(c * cols, (c + 1) * cols) for c in range(tokens // cols)]

    def first(unit, slot, chunk):
        t, h = unit
        at = slice(t * rows, (t + 1) * rows)
        kept[slot, chunk, :] = nt(kside[h, chunk, :], qside[h, at, :])
        dprobs[slot, chunk, :] = nt(vside[chunk, :], gside[h, at, :])

    for chunk in chunks:
        first(units[0], 0, chunk)
    for u, (t, h) in enumerate(units):
        at = slice(t * rows, (t + 1) * rows)
        dq = None
        for chunk in chunks:
            if u + 1 < len(units):
                first(units[u + 1], (u + 1) % 2, chunk)
            probs = jnp.exp2(kept[u % 2, chunk, :])
            dscores = (probs * dprobs[u % 2, chunk, :]).astype(BF16)
            dv, dk = nn(probs.astype(BF16), gside[h, at, 0:128]), nn(dscores, qhead[h, at, :])
            if u == 0:
                dvals[chunk, :] = dv
                dkeys[chunk, :] = dk
            else:
                dvals[chunk, :] += dv
                dkeys[chunk, :] += dk
            part = tn(dscores, k_ref[chunk, :])
            dq = part if dq is None else dq + part
        if h == 0:
            dquery[...] = dq
        else:
            out_ref[0, at, :] = (jnp.where(lane < 64, dquery[...], dq) * 0.125).astype(BF16)
    out_ref[1] = dkeys[...].astype(BF16)
    out_ref[2] = dvals[...].astype(BF16)


def attend_back(projected, g_mixed, mixed, lse, onehot, keymask):
    tokens = projected.shape[0]
    pairs = projected.shape[1] // 3 // 128
    part = lambda at: pl.BlockSpec((tokens, 128), lambda j: (0, at + j))
    whole = pl.BlockSpec((tokens, 128), lambda j: (0, 0))
    wide, narrow = pltpu.VMEM((2, tokens, 256), BF16), pltpu.VMEM((tokens, 128), F32)
    square_tile = pltpu.VMEM((2, tokens, tokens // 2), F32)
    return pl.pallas_call(
        attend_back_kernel,
        grid=(pairs,),
        in_specs=[part(0), part(pairs), part(2 * pairs), part(0), part(0), part(0), whole, whole],
        out_specs=pl.BlockSpec((3, tokens, 128), lambda j: (0, 0, j)),
        scratch_shapes=[
            wide, wide, pltpu.VMEM((tokens, 256), BF16), wide, pltpu.VMEM((2, tokens, 128), BF16),
            narrow, narrow, square_tile, square_tile, pltpu.VMEM((tokens // 2, 128), F32),
        ],
        out_shape=jax.ShapeDtypeStruct((3, tokens, pairs * 128), BF16),
        compiler_params=params(),
        cost_estimate=cost(5 * 2 * 12 * tokens * tokens * 256, tokens * 768 * 22, 12 * tokens * tokens),
        name="attend_back",
    )(projected, projected, projected, g_mixed, mixed, lse, onehot, keymask)


def mlp_kernel(
    embed_ref, mixed_ref, cot_ref, live_ref, small_ref, shift_ref, wo_ref, up_ref, down_ref,
    out_ref, ghid_ref, gmixed_ref, gdown_ref, gup_ref, gwo_ref, sums_ref, gshift_ref,
    hidden, xhats, norm2, gbranch, total, gnorm, act, gpre,
):
    step = pl.program_id(0)
    tokens = embed_ref.shape[0]

    @pl.when(step == 0)
    def _():
        def body(rows):
            value = embed_ref[rows, :] + nn(mixed_ref[rows, :], square(wo_ref)) + small_ref[4:5, :]
            hidden[rows, :] = value
            total[rows, :] = value + small_ref[6:7, :]
            xhat, _ = norm_parts(value)
            norm2[rows, :] = (xhat * small_ref[8:9, :] + small_ref[5:6, :]).astype(BF16)
            gbranch[rows, :] = (cot_ref[rows, :].astype(F32) * live_ref[rows, :]).astype(BF16)
            gnorm[rows, :] = jnp.zeros_like(value)

        row_tiles(tokens, body)

    up = square(up_ref)
    down = jnp.concatenate(
        [down_ref[r, f, 0] for f in range(down_ref.shape[1]) for r in range(down_ref.shape[0])]
    )

    def body(rows):
        x = nn(norm2[rows, :], up) + shift_ref[0]
        square_x = x * x
        t = jnp.tanh(0.7978845608028654 * (x + 0.044715 * (square_x * x)))
        half = 0.5 * (1.0 + t)
        acts = (x * half).astype(BF16)
        act[rows, :] = acts
        total[rows, :] += nn(acts, down)
        slope = half + 0.5 * x * (1.0 - t * t) * (
            0.7978845608028654 + (0.7978845608028654 * 3 * 0.044715) * square_x
        )
        gp = (nt(gbranch[rows, :], down) * slope).astype(BF16)
        gpre[rows, :] = gp
        gnorm[rows, :] += nt(gp, up)

    row_tiles(tokens, body)
    gdown_ref[0] = tn(act[...], gbranch[...]).astype(BF16)
    gup_ref[...] = tn(norm2[...], gpre[...]).astype(BF16).reshape(gup_ref.shape)
    gshift_ref[0] = jnp.sum(gpre[...].astype(F32), axis=0, keepdims=True)

    @pl.when(step == 3)
    def _():
        sums_ref[...] = jnp.zeros_like(sums_ref)
        wo = square(wo_ref)

        def body(rows):
            out_ref[rows, :] = (total[rows, :] * live_ref[rows, :]).astype(BF16)
            xhat, rstd = norm_parts(hidden[rows, :])
            grad = gnorm[rows, :]
            gout = gbranch[rows, :].astype(F32)
            ghid = gout + norm_back(xhat, rstd, grad, small_ref[8:9, :])
            ghid_ref[rows, :] = ghid
            gmix = ghid.astype(BF16)
            xhats[rows, :] = gmix
            gmixed_ref[rows, :] = nt(gmix, wo).astype(BF16)
            sums_ref[4:5, :] += jnp.sum(gmix.astype(F32), axis=0, keepdims=True)
            sums_ref[5:6, :] += jnp.sum(grad, axis=0, keepdims=True)
            sums_ref[6:7, :] += jnp.sum(gout, axis=0, keepdims=True)
            sums_ref[8:9, :] += jnp.sum(grad * xhat, axis=0, keepdims=True)

        row_tiles(tokens, body)
        gwo_ref[...] = tn(mixed_ref[...], xhats[...]).astype(BF16).reshape(gwo_ref.shape)


def mlp_call(embed, mixed, cotangent, live, small, shift, downs, colwise):
    tokens, width = embed.shape
    bands, deep = colwise.shape[1], colwise.shape[3]
    fixed = pl.BlockSpec((tokens, width), lambda s: (0, 0))
    whole = lambda a: pl.BlockSpec(a.shape, lambda s: (0, 0))
    band = lambda group, at: pl.BlockSpec((1, bands, 1, deep, width), lambda s: (at(s), 0, group, 0, 0))
    last = downs.shape[2] - 1
    down_block = (downs.shape[0], downs.shape[1] // 4, 1) + downs.shape[3:]
    scratch = lambda kind: pltpu.VMEM((tokens, width), kind)
    return pl.pallas_call(
        mlp_kernel,
        grid=(4,),
        in_specs=[
            fixed, fixed, fixed, whole(live), whole(small),
            pl.BlockSpec((1, 1, width), lambda s: (s, 0, 0)),
            band(0, lambda s: 3), band(1, lambda s: s),
            pl.BlockSpec(down_block, lambda s: (0, s, last, 0, 0)),
        ],
        out_specs=[
            fixed, fixed, fixed,
            pl.BlockSpec((1, width, width), lambda s: (s, 0, 0)),
            pl.BlockSpec((bands, 1, deep, width), lambda s: (0, s, 0, 0)),
            pl.BlockSpec((bands, deep, width), lambda s: (0, 0, 0)),
            pl.BlockSpec((16, width), lambda s: (0, 0)),
            pl.BlockSpec((1, 1, width), lambda s: (s, 0, 0)),
        ],
        out_shape=[
            jax.ShapeDtypeStruct((tokens, width), BF16),
            jax.ShapeDtypeStruct((tokens, width), F32),
            jax.ShapeDtypeStruct((tokens, width), BF16),
            jax.ShapeDtypeStruct((4, width, width), BF16),
            jax.ShapeDtypeStruct((bands, 4, deep, width), BF16),
            jax.ShapeDtypeStruct((bands, deep, width), BF16),
            jax.ShapeDtypeStruct((16, width), F32),
            jax.ShapeDtypeStruct((4, 1, width), F32),
        ],
        scratch_shapes=[
            scratch(F32), scratch(BF16), scratch(BF16), scratch(BF16),
            scratch(F32), scratch(F32), scratch(BF16), scratch(BF16),
        ],
        compiler_params=params(),
        cost_estimate=cost(27 * 2 * tokens * width * width, tokens * width * 20 + 18 * width * width * 2),
        name="mlp",
    )(embed, mixed, cotangent, live, small, shift, colwise, colwise, downs)


def store_split(core, value, mine_ref, other_ref):
    shape = mine_ref.shape
    pairs = value.reshape(-1, 2, shape[-2], shape[-1])
    first, second = pairs[:, 0].reshape(shape), pairs[:, 1].reshape(shape)

    @pl.when(core == 0)
    def _():
        mine_ref[...] = first
        other_ref[...] = second

    @pl.when(core != 0)
    def _():
        mine_ref[...] = second
        other_ref[...] = first


def qkv_grad_kernel(core_ref, norm_ref, dproj_ref, gwo_ref, mine_ref, other_ref):
    step = pl.program_id(0)

    @pl.when(step < 3)
    def _():
        value = tn(norm_ref[...], dproj_ref[0]).astype(BF16)
        store_split(core_ref[0], value, mine_ref, other_ref)

    @pl.when(step == 3)
    def _():
        store_split(core_ref[0], square(gwo_ref), mine_ref, other_ref)


def qkv_grad(core, normed1, dproj, g_out):
    tokens, width = normed1.shape
    bands, deep = g_out.shape[0], g_out.shape[1]
    half = (bands // 2, deep) if bands > 1 else (1, width // 2)
    pair = pl.BlockSpec((half[0], 1, half[1], width), lambda s, c: (0, s, 0, 0))
    shape = jax.ShapeDtypeStruct((half[0], 4, half[1], width), BF16)
    return pl.pallas_call(
        qkv_grad_kernel,
        grid_spec=pltpu.PrefetchScalarGridSpec(
            num_scalar_prefetch=1,
            grid=(4,),
            in_specs=[
                pl.BlockSpec((tokens, width), lambda s, c: (0, 0)),
                pl.BlockSpec((1, tokens, width), lambda s, c: (jnp.minimum(s, 2), 0, 0)),
                pl.BlockSpec(g_out.shape, lambda s, c: (0, 0, 0)),
            ],
            out_specs=[pair, pair],
        ),
        out_shape=[shape, shape],
        compiler_params=params(),
        cost_estimate=cost(1e6, 1e5),
        name="qkv_grad",
    )(core, normed1, dproj, g_out)


def embed_back_kernel(
    dproj_ref, qkv_ref, embed_ref, ghid_ref, pos_ref, small_ref, gemb_ref, gpos_ref, sums_ref, gnorm
):
    step = pl.program_id(0)
    tokens = embed_ref.shape[0]
    weight = square(qkv_ref)

    column = jnp.sum(dproj_ref[0].astype(F32), axis=0, keepdims=True)

    @pl.when(step == 0)
    def _():
        sums_ref[...] = jnp.zeros_like(sums_ref)
        sums_ref[2:3, :] = column

        def body(rows):
            gnorm[rows, :] = nt(dproj_ref[0, rows, :], weight)

        row_tiles(tokens, body)

    @pl.when(step == 1)
    def _():
        def body(rows):
            gnorm[rows, :] += nt(dproj_ref[0, rows, :], weight)

        row_tiles(tokens, body)

    @pl.when(step == 2)
    def _():
        sums_ref[3:4, :] = column

        def body(rows):
            grad = gnorm[rows, :] + nt(dproj_ref[0, rows, :], weight)
            xhat, rstd = norm_parts(embed_ref[rows, :])
            gemb = (ghid_ref[rows, :] + norm_back(xhat, rstd, grad, small_ref[7:8, :])).astype(BF16)
            gemb_ref[rows, :] = gemb
            sums_ref[0:1, :] += jnp.sum(gemb.astype(F32), axis=0, keepdims=True)
            sums_ref[1:2, :] += jnp.sum(grad, axis=0, keepdims=True)
            sums_ref[7:8, :] += jnp.sum(grad * xhat, axis=0, keepdims=True)

        row_tiles(tokens, body)
        gpos_ref[...] = tn(pos_ref[...], gemb_ref[...])


def embed_back(dproj, colwise, embed, g_hidden, pos_rows, small):
    tokens, width = embed.shape
    bands, deep = colwise.shape[1], colwise.shape[3]
    fixed = pl.BlockSpec((tokens, width), lambda s: (0, 0))
    whole = lambda a: pl.BlockSpec(a.shape, lambda s: (0, 0))
    return pl.pallas_call(
        embed_back_kernel,
        grid=(3,),
        in_specs=[
            pl.BlockSpec((1, tokens, width), lambda s: (s, 0, 0)),
            pl.BlockSpec((1, bands, 1, deep, width), lambda s: (s, 0, 0, 0, 0)),
            fixed, fixed, whole(pos_rows), whole(small),
        ],
        out_specs=[
            fixed, pl.BlockSpec((128, width), lambda s: (0, 0)), pl.BlockSpec((16, width), lambda s: (0, 0)),
        ],
        out_shape=[
            jax.ShapeDtypeStruct((tokens, width), BF16),
            jax.ShapeDtypeStruct((128, width), F32),
            jax.ShapeDtypeStruct((16, width), F32),
        ],
        scratch_shapes=[pltpu.VMEM((tokens, width), F32)],
        compiler_params=params(),
        cost_estimate=cost(1e6, 1e5),
        name="embed_back",
    )(dproj, colwise, embed, g_hidden, pos_rows, small)


def patch_grad_kernel(core_ref, res_ref, g_ref, small_ref, mine_ref, other_ref):
    shard = mine_ref.shape[1] - small_ref.shape[1]
    value = tn(res_ref[...], g_ref[...]).astype(BF16).reshape(-1, 2, shard, mine_ref.shape[2])
    tail = small_ref[...].reshape(-1, 2, small_ref.shape[1], small_ref.shape[2])

    def store(ref, which):
        ref[:, 0:shard, :] = value[:, which]
        ref[:, shard:, :] = tail[:, which]

    @pl.when(core_ref[0] == 0)
    def _():
        store(mine_ref, 0)
        store(other_ref, 1)

    @pl.when(core_ref[0] != 0)
    def _():
        store(mine_ref, 1)
        store(other_ref, 0)


def patch_grad(core, resized, g_emb, g_small):
    tokens, width = g_emb.shape
    owners, packed = g_small.shape[0], g_small.shape[1]
    shard = 4 * width // owners
    pair = pl.BlockSpec((owners // 8, shard + packed, width), lambda s, c: (s, 0, 0))
    shape = jax.ShapeDtypeStruct((owners // 2, shard + packed, width), BF16)
    return pl.pallas_call(
        patch_grad_kernel,
        grid_spec=pltpu.PrefetchScalarGridSpec(
            num_scalar_prefetch=1,
            grid=(4,),
            in_specs=[
                pl.BlockSpec((tokens, width), lambda s, c: (0, s)),
                pl.BlockSpec((tokens, width), lambda s, c: (0, 0)),
                pl.BlockSpec((owners // 4, packed, width), lambda s, c: (s, 0, 0)),
            ],
            out_specs=[pair, pair],
        ),
        out_shape=[shape, shape],
        compiler_params=params(),
        cost_estimate=cost(1e6, 1e5),
        name="patch_grad",
    )(core, resized, g_emb, g_small)


def finish_kernel(
    kern_ref, rest_ref, up_ref, down_ref,
    o_kern, o_qkv, o_out, o_up, o_down, o_biases, o_gains, o_pos, o_shift,
):
    shard, width = o_kern.shape
    depth = o_out.shape[0]
    kern = kern_ref[...].astype(F32)
    o_kern[...] = kern[0:shard]
    o_down[...] = down_ref[...].astype(F32)
    rest, up = rest_ref[...].astype(F32), up_ref[...].astype(F32)
    for j in range(4):
        rows, columns = slice(j * depth, (j + 1) * depth), slice(j * width, (j + 1) * width)
        o_up[:, columns] = up[rows]
        if j < 3:
            o_qkv[:, columns] = rest[rows]
        else:
            o_out[...] = rest[rows]
    small = jnp.concatenate([kern[shard:, 0:128], kern[shard:, 128:256]])[:, 0:depth]
    at = 0
    for ref in (o_biases, o_gains, o_pos, o_shift):
        ref[...] = small[at : at + ref.shape[0]]
        at += ref.shape[0]


def finish(kern, rest, up, down, cells):
    shard, width = down.shape
    depth = shard // 4
    shapes = [
        (shard, width), (depth, 3 * width), (depth, width), (depth, 4 * width), (shard, width),
        (7, depth), (2, depth), (cells, depth), (4, depth),
    ]
    return pl.pallas_call(
        finish_kernel,
        out_shape=[jax.ShapeDtypeStruct(shape, F32) for shape in shapes],
        compiler_params=params(),
        name="finish",
    )(kern, rest, up, down)


def bit_of(axis, bit):
    return (lax.axis_index(axis) >> bit) & 1


class Sum:
    def __init__(self, mine, other, reps, owners, steps):
        self.sizes = dict(rep=reps, fsdp=owners)
        self.lead = [("fsdp", b) for b in range(1, owners.bit_length() - 1)][::-1]
        self.steps = [("fsdp", 0)] + steps
        self.back = [s for s in steps if s[0] == "rep"][::-1]
        shape = (2,) * len(self.lead) + mine.shape[1:]
        self.launch(mine.reshape(shape), other.reshape(shape))

    def launch(self, kept, sent):
        axis, bit = (self.steps or self.back)[0]
        pairs = [(i, i ^ (1 << bit)) for i in range(self.sizes[axis])]
        kept, sent = lax.optimization_barrier((kept, sent))
        self.kept, self.flying = kept, lax.ppermute(sent, axis, pairs)

    def land(self):
        if not self.steps and not self.back:
            return
        if self.steps:
            self.steps.pop(0)
            value = (self.kept.astype(F32) + self.flying.astype(F32)).astype(BF16)
        else:
            axis, bit = self.back.pop(0)
            low = bit_of(axis, bit) == 0
            a, b = self.kept, self.flying
            value = jnp.concatenate([jnp.where(low, a, b), jnp.where(low, b, a)])
        if self.steps:
            axis, bit = self.steps[0]
            if axis == "fsdp":
                at = self.lead.index((axis, bit))
                self.lead.remove((axis, bit))
            else:
                at = len(self.lead)
                value = value.reshape(value.shape[:at] + (2, value.shape[at] // 2) + value.shape[at + 1 :])
            mine = bit_of(axis, bit)
            pick = lambda i: lax.dynamic_index_in_dim(value, i, at, keepdims=False)
            self.launch(pick(mine), pick(1 - mine))
        elif self.back:
            self.launch(value, value)
        else:
            self.kept = value

    def total(self):
        while self.steps or self.back:
            self.land()
        return self.kept


class Gather:
    def __init__(self, shard, reps, owners, flip=False):
        rep, own = reps.bit_length() - 1, owners.bit_length() - 1
        self.sizes = dict(rep=reps, fsdp=owners)
        self.order = [("fsdp", b) for b in range(own)][::-1] + [("rep", b) for b in range(rep)][::-1]
        over_reps = self.order[own:][::-1] if flip else self.order[own:]
        self.steps = self.order[: own - 1] + over_reps + [("fsdp", 0)]
        self.held = []
        self.shape = (owners * shard.shape[0], shard.shape[1])
        share = shard.shape[0] // reps
        at = lax.axis_index("rep") * share if reps > 1 else 0
        self.launch(lax.dynamic_slice(shard, (at, 0), (share, shard.shape[1])))

    def launch(self, value):
        self.kept = value
        if self.steps:
            axis, bit = self.steps[0]
            self.flying = lax.ppermute(value, axis, [(i, i ^ (1 << bit)) for i in range(self.sizes[axis])])

    def land(self):
        if not self.steps:
            return
        axis, bit = self.steps.pop(0)
        at = sum(self.order.index(h) < self.order.index((axis, bit)) for h in self.held)
        self.held.append((axis, bit))
        low = bit_of(axis, bit) == 0
        a, b = self.kept, self.flying
        self.launch(jnp.stack([jnp.where(low, a, b), jnp.where(low, b, a)], axis=at))

    def total(self):
        while self.steps:
            self.land()
        return self.kept.reshape(self.shape)


def beside(sums, work, value):
    value = lax.optimization_barrier((value, *[one.kept for one in sums]))[0]
    value, *kept = lax.optimization_barrier((work(value), *[one.kept for one in sums]))
    for one, k in zip(sums, kept):
        one.kept = k
    return value


def local(reps, owners, *arrays):
    (
        pixels, image_class, resize_a, resize_b, resize_c, posmap_a, posmap_b, posmap_c, cotangent,
        patch_kernel, pos_table, qkv_weight, out_weight, up_weight, down_weight, biases, up_bias, gains,
    ) = arrays
    tokens = pixels.shape[0]
    width = out_weight.shape[1]
    depth = out_weight.shape[0]
    shard = patch_kernel.shape[0]
    cells = pos_table.shape[0]
    slots = image_class.shape[1]

    def stacked(shards):
        return jnp.concatenate([w.reshape(depth, -1, width).transpose(1, 0, 2) for w in shards]).reshape(shard, width)

    small_here = jnp.concatenate([biases, gains, pos_table, up_bias.reshape(-1, depth)])
    here_rows = small_here.shape[0]
    small_here = jnp.pad(small_here, ((0, -here_rows % 16), (0, 0)))
    bundle = jnp.stack([stacked([qkv_weight, out_weight]), stacked([up_weight]), down_weight])
    share = shard // reps
    here = lax.dynamic_slice(bundle, (0, lax.axis_index("rep") * share, 0), (3, share, width))
    groups = lax.all_gather(here, ("rep", "fsdp"), axis=0, tiled=False).reshape(reps, owners, 3, share, width)
    kernel = Gather(patch_kernel, reps, owners)
    little = Gather(small_here, 1, owners)
    while len(kernel.steps) > 2:
        kernel.land()
        little.land()
    small_all = little.total().reshape(owners, -1, depth)[:, :here_rows]
    if reps == 4 and depth % 16 == 0 and owners % 4 == 0:
        colwise = downs = groups
    else:
        groups = groups.transpose(2, 1, 0, 3, 4).reshape(3, owners, shard, width)
        colwise = groups.reshape(3, owners, 4, depth, width).transpose(2, 0, 1, 3, 4).reshape(4, 1, 3, width, width)
        downs = groups[2].reshape(1, 4, 1, width, width)
    rows_of = small_all[:, : 9 + cells].transpose(1, 0, 2).reshape(9 + cells, width)
    small = jnp.pad(rows_of[:9].astype(F32), ((0, 7), (0, 0)))
    table = jnp.pad(rows_of[9:], ((0, 128 - cells), (0, 0)))
    shift = small_all[:, 9 + cells :].reshape(4, 1, width).astype(F32)

    segment, category, offset, live_rows = token_layout(image_class[0], tokens)
    live = live_rows[:, None].astype(F32)
    lists = chunk_lists(category)
    lane = jnp.arange(128, dtype=jnp.int32)[None, :]
    same = segment[:, None] == lane
    onehot = same.astype(BF16)
    keymask = jnp.where(
        lane <= slots, jnp.where(same, 0.0, NEG), jnp.where((lane >= 64) & (lane < 67), -1.0, 0.0)
    ).astype(BF16)
    maps = jnp.concatenate([posmap_a, posmap_b, posmap_c, jnp.zeros((1, cells), BF16)])
    maps = jnp.pad(maps, ((0, 0), (0, 128 - cells)))
    first = jnp.array([0, GRID_A * GRID_A, GRID_A * GRID_A + GRID_B * GRID_B], jnp.int32)
    at = jnp.where(category < 3, first[jnp.minimum(category, 2)] + offset, maps.shape[0] - 1)
    pos_rows = jnp.take(maps, at, axis=0)
    cats = category[:, None]
    ra = jnp.pad(resize_a, ((0, -resize_a.shape[0] % 128), (0, 0)))
    rb = jnp.pad(resize_b, ((0, -resize_b.shape[0] % 128), (0, 0)))

    pixels, pos_rows, live, onehot, keymask, small, table, shift = lax.optimization_barrier(
        (pixels, pos_rows, live, onehot, keymask, small, table, shift)
    )
    resized = beside([kernel], lambda p: resize(lists, p, cats, ra, rb, resize_c), pixels)
    patch = kernel.total()
    embed, normed1 = embed_call(resized, patch, pos_rows, table, small)
    projected = project(normed1, colwise, small)
    mixed, lse = attend(projected, onehot, keymask)
    output, g_hidden, g_mixed, g_down, g_up, g_out, sums_mlp, g_shift = mlp_call(
        embed, mixed, cotangent, live, small, shift, downs, colwise
    )
    def bands_of(blocks, number):
        if blocks.shape[0] != owners:
            blocks = blocks.reshape(number, owners, depth, width).transpose(1, 0, 2, 3)
        return blocks.reshape(owners, number * depth, width)

    scatter = lambda x: lax.psum_scatter(x, "fsdp", scatter_dimension=0, tiled=False)
    s_down = scatter(g_down.reshape(owners, shard, width))
    s_up = scatter(bands_of(g_up, 4))
    dproj = attend_back(projected, g_mixed, mixed, lse, onehot, keymask)
    core = bit_of("fsdp", 0).reshape(1)
    own, rep = owners.bit_length() - 1, reps.bit_length() - 1
    others = [("fsdp", b) for b in range(1, own)]
    over_reps = [("rep", b) for b in range(rep)]
    g_emb, g_pos, sums_embed = embed_back(dproj, colwise, embed, g_hidden, pos_rows, small)
    lanes = ((0, 0), (0, 0), (0, 128 - depth))
    g_small = jnp.concatenate([(sums_mlp + sums_embed)[:9], g_pos[:cells]]).reshape(9 + cells, owners, depth)
    g_small = jnp.concatenate(
        [jnp.pad(g_small, lanes).transpose(1, 0, 2), jnp.pad(g_shift.reshape(owners, 4, depth), lanes)], axis=1
    ).astype(BF16)
    g_small = jnp.pad(g_small, ((0, 0), (0, 64 - g_small.shape[1]), (0, 0)))
    g_small = jnp.concatenate([g_small[:, :32], g_small[:, 32:], jnp.zeros((owners, 32, width - 256), BF16)], axis=2)
    mine, other = patch_grad(core, resized, g_emb, g_small)
    kern = Sum(mine, other, reps, owners, over_reps[::-1] + others)
    mine, other = beside([kern], lambda d: qkv_grad(core, normed1, d, g_out), dproj)
    kern.land()
    if g_out.shape[0] == 1:
        both = jnp.concatenate([jnp.where(core == 0, mine, other), jnp.where(core == 0, other, mine)], axis=2)
        both = both.reshape(4, owners // 2, 2, depth, width).transpose(2, 1, 0, 3, 4)
        mine, other = jnp.where(core == 0, both[0], both[1]), jnp.where(core == 0, both[1], both[0])
    halves = (owners // 2, shard, width)
    qkvo = Sum(mine.reshape(halves), other.reshape(halves), reps, owners, over_reps[:1] + others + over_reps[1:])

    kern.kept, qkvo.kept = lax.optimization_barrier((kern.kept, qkvo.kept))
    qkvo.land()
    g_emb = lax.optimization_barrier((g_emb, s_down))[0]
    grad_pixels = None
    for channel in range(3):

        def work(pair):
            return unresize(
                lists, pair[0], patch, cats, ra, rb, resize_c, pixels.shape[1] // 3, channel, 0, 1, pair[1]
            )

        if channel == 1:
            g_emb = lax.optimization_barrier((g_emb, s_up))[0]
        grad_pixels = beside([qkvo, kern], work, (g_emb, grad_pixels))
        kern.land()
        qkvo.land()
    s_up, s_down = (lax.psum(p, "rep") for p in (s_up, s_down))
    while len(kern.back) > 1 or kern.steps:
        kern.land()
        qkvo.land()
    kern.kept, s_up, s_down = lax.optimization_barrier((kern.kept, s_up, s_down))
    totals = finish(kern.total(), qkvo.total(), s_up, s_down, cells)
    t_kernel, t_qkv, t_out, t_up, t_down, t_biases, t_gains, t_pos, t_shift = totals
    return (
        output, grad_pixels, t_kernel, t_pos, t_qkv, t_out, t_up, t_down, t_biases, t_shift.reshape(-1), t_gains
    )


def solution(mesh):
    tokens = P(("rep", "fsdp"), None)
    rows, columns = P("fsdp", None), P(None, "fsdp")
    in_specs = (
        tokens, tokens, P(), P(), P(), P(), P(), P(), tokens,
        rows, columns, rows, rows, rows, rows, columns, P("fsdp"), columns,
    )
    out_specs = (tokens, tokens, rows, columns, rows, rows, rows, rows, columns, P("fsdp"), columns)
    reps, owners = mesh.shape["rep"], mesh.shape["fsdp"]

    def here(*arrays):
        return local(reps, owners, *arrays)

    return jax.shard_map(here, mesh=mesh, in_specs=in_specs, out_specs=out_specs, check_vma=False)
```
